768 devices in a mesh: nodes: 64 (over y, x, core), feat: 12 (over z).
Axes of the slice: x: 4, y: 8, z: 12, core: 2. Of those that a mesh axis runs over, the one named last changes fastest.
Arguments:
- features: bfloat16 [65536, 1152], P('nodes', 'feat'), may hold values from -6 to 6
- w_neigh: bfloat16 [1152, 256], P('feat'), may hold values from -0.1875 to 0.1875
- w_self: bfloat16 [1152, 256], P('feat'), may hold values from -0.1875 to 0.1875
- bias: float32 [256], replicated, may hold values from -3 to 3
- target_blocks: int32 [384], P('nodes'), may hold values from 0 to 7, as said below
- loc_tiles: bfloat16 [384, 8, 128, 128], P('nodes'), may hold values from -0.25 to 0.25
- loc_src: int32 [384, 8], P('nodes'), may hold values from 0 to 7
- loc_count: int32 [384], P('nodes'), may hold values from 1 to 8, as said below
- rem_tiles: bfloat16 [64, 64, 128, 128], P('nodes'), may hold values from -0.25 to 0.25
- rem_src: int32 [64, 64], P('nodes'), may hold values from 0 to 7
- rem_slot: int32 [64, 64], P('nodes'), may hold values from 0 to 5
- degree: int32 [49152], P('nodes'), may hold values from 1 to 8
- cotangent: bfloat16 [49152, 256], P(('nodes', 'feat')), may hold values from -6 to 6
Outputs:
- activation: bfloat16 [49152, 256], P(('nodes', 'feat'))
- grad_neigh: float32 [1152, 256], P('feat')
- grad_self: float32 [1152, 256], P('feat')
- grad_bias: float32 [256], replicated
The draws below stay inside these ranges and needn't reach their ends.
Inputs may be any that keep to these rules, and one draw needn't show every extreme that they name: `target_blocks`: the 6 ids of one index of nodes are distinct local block ids. Tiles k < loc_count[t] of target block t are in use, the others are ignored.
All inputs are finite; a program needn't handle non-finite values.
Results may differ from the reference program's by a relative error of at most 0.007.
Values may be sent and summed in bfloat16 or wider, within the bound.
A program may use at most 32 MiB of HBM per device.

```python
import jax
import jax.numpy as jnp
from jax import lax

BLOCK = 128
H = 256
LOC = 8
DEGMAX = 8
NB_DEV = 8
TGT_DEV = 6
F = 1152
BLOCKS = 512
NODES = 65536
TARGETS = 384
ROWS = 49152
N_NODES = 64


def draw_target_blocks(key, part):
    key = jax.random.fold_in(key, 11)
    subkeys = jax.random.split(key, N_NODES)
    chosen = jax.vmap(lambda k: jax.random.permutation(k, NB_DEV)[:TGT_DEV])(subkeys)
    return chosen.reshape(-1).astype(jnp.int32)


def draw_loc_count(key, part):
    key = jax.random.fold_in(key, 23)
    counts = jax.random.randint(key, (TARGETS,), 1, LOC + 1)
    counts = counts.at[0].set(LOC)
    return counts.astype(jnp.int32)


def set_ends(values, key, least, high):
    extent = values.shape
    spot = [jax.random.randint(jax.random.fold_in(key, axis), (), 0, extent[axis]) for axis in range(len(extent))]
    values = values.at[tuple(spot)].set(least)
    longest = extent.index(max(extent))
    spot[longest] = (spot[longest] + 1) % extent[longest]
    return values.at[tuple(spot)].set(high)


def shard_levels(key, shape, cuts, least, high):
    loudness, own = 1.0, jax.random.fold_in(key, 6)
    for dim, parts in cuts:
        steps = jnp.exp(jax.random.uniform(jax.random.fold_in(own, dim), (parts,), jnp.float32, least / len(cuts), high / len(cuts)))
        loudness = loudness * jnp.repeat(steps, shape[dim] // parts).reshape([-1 if axis == dim else 1 for axis in range(len(shape))])
    return loudness


def scatter_about(key, extent, spread, limit, shards=(), held_as=jnp.bfloat16):
    entries = spread * jax.random.normal(key, extent, jnp.float32)
    if shards:
        entries = entries * shard_levels(key, extent, shards, -0.22, 0.18)
    return jnp.clip(entries, -limit, limit).astype(held_as)


def setup_inputs(seed: int = 0) -> dict:
    arg_keys = jax.random.split(jax.random.key(seed), 14)
    features = scatter_about(arg_keys[0], (NODES, F), 1.0, 6.0, ((0, 64), (1, 12)))
    w_neigh = scatter_about(arg_keys[1], (F, H), F ** -0.5, 0.1875, ((0, 12),))
    w_self = scatter_about(arg_keys[2], (F, H), F ** -0.5, 0.1875, ((0, 12),))
    bias = scatter_about(arg_keys[3], (H,), 0.5, 3.0, (), jnp.float32)
    target_blocks = draw_target_blocks(jax.random.fold_in(arg_keys[13], 71), 0)
    loc_tiles = scatter_about(arg_keys[5], (TARGETS, LOC, BLOCK, BLOCK), (BLOCK * LOC // 2) ** -0.5, 0.25, ((0, 64),))
    loc_src = set_ends(jax.random.randint(arg_keys[6], (TARGETS, LOC), 0, NB_DEV), jax.random.fold_in(arg_keys[6], 1), 0, NB_DEV - 1).astype(jnp.int32)
    loc_count = draw_loc_count(jax.random.fold_in(arg_keys[13], 71), 0)
    rem_tiles = scatter_about(arg_keys[8], (N_NODES, N_NODES, BLOCK, BLOCK), (BLOCK * LOC // 2) ** -0.5, 0.25, ((0, 64),))
    rem_src = set_ends(jax.random.randint(arg_keys[9], (N_NODES, N_NODES), 0, NB_DEV), jax.random.fold_in(arg_keys[9], 1), 0, NB_DEV - 1).astype(jnp.int32)
    rem_slot = set_ends(jax.random.randint(arg_keys[10], (N_NODES, N_NODES), 0, TGT_DEV), jax.random.fold_in(arg_keys[10], 1), 0, TGT_DEV - 1).astype(jnp.int32)
    degree = set_ends(jax.random.randint(arg_keys[11], (ROWS,), 1, DEGMAX + 1), jax.random.fold_in(arg_keys[11], 1), 1, DEGMAX).astype(jnp.int32)
    cotangent = scatter_about(arg_keys[12], (ROWS, H), 1.0, 6.0, ((0, 768),))
    return {"features": features, "w_neigh": w_neigh, "w_self": w_self, "bias": bias, "target_blocks": target_blocks, "loc_tiles": loc_tiles, "loc_src": loc_src, "loc_count": loc_count, "rem_tiles": rem_tiles, "rem_src": rem_src, "rem_slot": rem_slot, "degree": degree, "cotangent": cotangent}


def gelu_slope(pre_act, upstream):
    _, pullback = jax.vjp(lambda value: jax.nn.gelu(value, approximate=True), pre_act)
    return pullback(upstream)[0]

def reference(features, w_neigh, w_self, bias, target_blocks, loc_tiles, loc_src, loc_count, rem_tiles, rem_src, rem_slot, degree, cotangent):
    blocks = features.reshape(N_NODES, NB_DEV, BLOCK, F)
    slot_ids = jnp.arange(TGT_DEV, dtype=jnp.int32)

    def add_source(carry, source):
        chosen = blocks[source][rem_src[source]]
        message = jnp.einsum('dij,djf->dif', rem_tiles[source].astype(jnp.float32), chosen.astype(jnp.float32)).astype(jnp.bfloat16)
        landing = (rem_slot[:, source][:, None] == slot_ids[None, :]).astype(jnp.float32)
        return (carry + jnp.einsum('dt,dif->dtif', landing, message.astype(jnp.float32)), None)
    start = jnp.zeros((N_NODES, TGT_DEV, BLOCK, F), jnp.float32)
    remote, _ = lax.scan(add_source, start, jnp.arange(N_NODES, dtype=jnp.int32))
    tiles_by_dev = loc_tiles.reshape(N_NODES, TGT_DEV, LOC, BLOCK, BLOCK)
    src_by_dev = loc_src.reshape(N_NODES, TGT_DEV, LOC)
    count_by_dev = loc_count.reshape(N_NODES, TGT_DEV)

    def nearby_sum(device):
        in_use = jnp.arange(LOC, dtype=jnp.int32)[None, :] < count_by_dev[device][:, None]
        masked = jnp.where(in_use[:, :, None, None], tiles_by_dev[device], jnp.zeros((), jnp.bfloat16))
        gathered = blocks[device][src_by_dev[device]]
        return jnp.einsum('tkij,tkjf->tif', masked.astype(jnp.float32), gathered.astype(jnp.float32))
    nearby = lax.map(nearby_sum, jnp.arange(N_NODES, dtype=jnp.int32))
    summed = (nearby + remote).reshape(ROWS, F)
    aggregated = (summed / degree.astype(jnp.float32)[:, None]).astype(jnp.bfloat16)
    flat_index = (jnp.arange(N_NODES, dtype=jnp.int32)[:, None] * NB_DEV + target_blocks.reshape(N_NODES, TGT_DEV)).reshape(-1)
    own_rows = features.reshape(BLOCKS, BLOCK, F)[flat_index].reshape(ROWS, F)
    pre_act = jnp.dot(aggregated, w_neigh, preferred_element_type=jnp.float32) + jnp.dot(own_rows, w_self, preferred_element_type=jnp.float32) + bias
    activation = jax.nn.gelu(pre_act, approximate=True).astype(jnp.bfloat16)
    slopes = gelu_slope(pre_act, cotangent.astype(jnp.float32)).astype(jnp.bfloat16)
    grad_neigh = jnp.dot(aggregated.T, slopes, preferred_element_type=jnp.float32)
    grad_self = jnp.dot(own_rows.T, slopes, preferred_element_type=jnp.float32)
    grad_bias = lax.optimization_barrier(jnp.sum(slopes.astype(jnp.float32), axis=0))
    return (activation, grad_neigh, grad_self, grad_bias)
```

```python
import functools

import jax
import jax.numpy as jnp
from jax import lax
from jax.experimental import pallas as pl
from jax.experimental.pallas import tpu as pltpu
from jax.sharding import PartitionSpec as P

BF = jnp.bfloat16
F32 = jnp.float32
MESH = pl.DeviceIdType.MESH
BLK = 128
HALF = 64
ROW_SIZE = 8


def dot_nt(a, b):
    return lax.dot_general(a, b, (((1,), (1,)), ((), ())), preferred_element_type=F32)


def dot_tn(a, b):
    return lax.dot_general(a, b, (((0,), (0,)), ((), ())), preferred_element_type=F32)


def loop(low, high, body):
    lax.fori_loop(low, high, lambda i, carry: (body(i), carry)[1], 0)


def pack_halves(block):
    mid = block.shape[0] // 2
    top, bottom = block[:mid], block[mid:]
    first = jnp.concatenate([top[:, :HALF], bottom[:, :HALF]], axis=1)
    second = jnp.concatenate([top[:, HALF:], bottom[:, HALF:]], axis=1)
    return first, second


def kernel(
    row,
    feat_hbm, wn_hbm, ws_hbm, bias_ref, tb, loct_hbm, lsrc, lcnt, remt_hbm, rsrc, rslot, deg_ref, cot_ref,
    act_ref, gn_ref, gs_ref, gb_ref,
    feat_v, xt, remt, loct, sb, rb, near, pacc, slot_v, slot_m, ring_out, ring_in,
    own_t, agg_t, own_s, own_r, agg_s, agg_r, wall, sl,
    ar_g, ar_r, ar_sum, ar_y, ar_t, ar_full,
    ld, ld_rem, row_ss, row_rs, slot_ss, slot_rs, ring_ss, ring_rs,
    own_ss, own_rs, agg_ss, agg_rs, w_ss, w_rs, wc_ss, wc_rs, sl_ss, sl_rs,
    a_ss, a_rs, b_ss, b_rs, c_ss, c_rs, d_ss, d_rs,
):
    n = lax.axis_index("nodes")
    z = lax.axis_index("feat")
    nodes = lax.axis_size("nodes")
    zs = lax.axis_size("feat")
    col = nodes // row
    reach = col // 2
    last = col - 1
    y = lax.div(n, row)
    g = lax.rem(n, row)
    core = lax.rem(g, 2)
    targets = near.shape[0]
    fw = xt.shape[1]
    mid = fw // 2
    nblocks = xt.shape[0]

    def row_peer(r):
        return y * row + lax.rem(g + r, row)

    def col_peer(k):
        return lax.rem(y + k, col) * row + g

    def z_peer(k):
        return lax.rem(z + k, zs)

    def delta(p):
        return (reach - (p + 1) // 2) * (2 * (p % 2) - 1)

    def to_node(src, dst, ssem, rsem, node):
        return pltpu.make_async_remote_copy(
            src_ref=src, dst_ref=dst, send_sem=ssem, recv_sem=rsem, device_id={"nodes": node}, device_id_type=MESH
        )

    def to_feat(src, dst, ssem, rsem, peer):
        return pltpu.make_async_remote_copy(
            src_ref=src, dst_ref=dst, send_sem=ssem, recv_sem=rsem, device_id={"feat": peer}, device_id_type=MESH
        )

    barrier = pltpu.get_barrier_semaphore()
    for r in range(1, row):
        pl.semaphore_signal(barrier, inc=1, device_id={"nodes": row_peer(r)}, device_id_type=MESH)
    for k in range(1, col):
        pl.semaphore_signal(barrier, inc=1, device_id={"nodes": col_peer(k)}, device_id_type=MESH)
    for k in range(1, zs):
        pl.semaphore_signal(barrier, inc=1, device_id={"feat": z_peer(k)}, device_id_type=MESH)

    load_feat = pltpu.make_async_copy(feat_hbm, feat_v, ld.at[0])
    load_feat.start()

    def dest_row(p):
        return lax.rem(y + delta(p) + col, col)

    def load_rem(p):
        return pltpu.make_async_copy(remt_hbm.at[0, pl.ds(dest_row(p) * row, row)], remt.at[p], ld_rem.at[p])

    for p in range(col):
        load_rem(p).start()
    load_loc = pltpu.make_async_copy(loct_hbm, loct, ld.at[1])
    load_loc.start()
    load_wn = pltpu.make_async_copy(wn_hbm, wall.at[0, z], ld.at[2])
    load_ws = pltpu.make_async_copy(ws_hbm, wall.at[1, z], ld.at[2])

    @pl.when(core == 0)
    def _():
        load_wn.start()

    @pl.when(core == 1)
    def _():
        load_ws.start()

    slot_v[0] = jnp.zeros(slot_v.shape[1:], jnp.int32)
    slot_v[0, 0:1, 0:nodes] = rslot[...]

    load_feat.wait()
    for b in range(nblocks):
        xt[b] = feat_v[b * BLK : (b + 1) * BLK, :].astype(F32).T.astype(BF)
    for j in range(targets):
        block = xt[tb[j]]
        own_t[j] = block
        first, second = pack_halves(block)
        own_s[2 * j] = first
        own_s[2 * j + 1] = second
    own_r[z] = own_s[z]

    def messages(p):
        load_rem(p).wait()
        yd = dest_row(p)
        for r in range(row):
            gd = lax.rem(g + r, row)
            block = xt[rsrc[0, yd * row + gd]]
            message = dot_nt(block, remt[p, gd]).astype(BF)
            if r == 0:
                rb[0, p] = message
            else:
                sb[r, p] = message

    def row_copy(r, p):
        return to_node(sb.at[r, p], rb.at[r, p], row_ss.at[r, p], row_rs.at[r, p], row_peer(r))

    messages(0)
    pl.semaphore_wait(barrier, row + col + zs - 3)

    def slot_copy(k):
        return to_node(slot_v.at[0], slot_v.at[k], slot_ss.at[k], slot_rs.at[k], col_peer(k))

    def own_copy(k):
        return to_feat(own_s.at[z_peer(k)], own_r.at[z], own_ss.at[k], own_rs.at[k], z_peer(k))

    def w_copy(k):
        return to_feat(wall.at[core, z], wall.at[core, z], w_ss.at[k], w_rs.at[k], z_peer(k))

    for r in range(1, row):
        row_copy(r, 0).start()
    for k in range(1, col):
        slot_copy(k).start()

    @pl.when(core == 0)
    def _():
        load_wn.wait()

    @pl.when(core == 1)
    def _():
        load_ws.wait()

    for k in range(1, zs):
        w_copy(k).start()

    def more(p):
        messages(p)
        for r in range(1, row):
            row_copy(r, p).start()

    loop(1, col, more)
    for k in range(1, zs):
        own_copy(k).start()

    load_loc.wait()

    def nearby(t):
        total = jnp.zeros((fw, BLK), F32)
        for k in range(lsrc.shape[1]):
            block = xt[lsrc[t, k]]
            block = jnp.where(k < lcnt[t], block, jnp.zeros_like(block))
            total = total + dot_nt(block, loct[t, k])
        near[t] = total

    loop(0, targets, nearby)

    for k in range(1, col):
        slot_copy(k).wait_recv()
    slots = pltpu.make_async_copy(slot_v, slot_m, ld.at[3])
    slots.start()
    slots.wait()

    def collapse(p, j, start):
        k = lax.rem(col - delta(p), col)
        total = start
        for r in range(row):
            source = y * row + lax.rem(g - r + row, row)
            hit = slot_m[k, 0, source] == j
            message = rb[r, p].astype(F32)
            total = total + jnp.where(hit, message, jnp.zeros_like(message))
        return total

    def row_wait(p):
        for r in range(1, row):
            row_copy(r, p).wait_recv()

    up = lax.rem(y + 1, col) * row + g
    down = lax.rem(y + col - 1, col) * row + g
    sides = (up, down)

    def ring_first(side):
        rows = pl.ds(side * mid, mid)
        return to_node(
            ring_out.at[0, :, rows], ring_in.at[side, 0, :, rows], ring_ss.at[side, 0], ring_rs.at[side, 0], sides[side]
        )

    def ring_copy(p):
        side, step = (p - 1) % 2, (p - 1) // 2 + 1
        return to_node(
            ring_out.at[p], ring_in.at[side, step], ring_ss.at[side, step], ring_rs.at[side, step], sides[side]
        )

    def ring_wait(side, step):
        if step == 0:
            ring_first(side).wait_recv()
        else:
            ring_copy(2 * step - 1 + side).wait_recv()

    row_wait(0)

    def start_ring(j):
        ring_out[0, j] = collapse(0, j, jnp.zeros((fw, BLK), F32)).astype(BF)

    loop(0, targets, start_ring)
    ring_first(0).start()
    ring_first(1).start()

    for p in range(1, last):
        side, step = (p - 1) % 2, (p - 1) // 2
        row_wait(p)

        def partial(j, p=p):
            pacc[j] = collapse(p, j, jnp.zeros((fw, BLK), F32))

        loop(0, targets, partial)
        ring_wait(side, step)

        def merge(j, p=p, side=side, step=step):
            if step == 0:
                own = pl.ds(side * mid, mid)
                other = pl.ds((1 - side) * mid, mid)
                ring_out[p, j, own] = (pacc[j, own] + ring_in[side, 0, j, own].astype(F32)).astype(BF)
                ring_out[p, j, other] = pacc[j, other].astype(BF)
            else:
                ring_out[p, j] = (pacc[j] + ring_in[side, step, j].astype(F32)).astype(BF)

        loop(0, targets, merge)
        ring_copy(p).start()

    partner = n + 1 - 2 * core

    def w_hand():
        return to_node(wall.at[core], wall.at[core], wc_ss.at[0], wc_rs.at[0], partner)

    def w_take():
        return to_node(wall.at[1 - core], wall.at[1 - core], wc_ss.at[0], wc_rs.at[0], partner)

    for k in range(1, zs):
        w_copy(k).wait_recv()
    w_hand().start()

    row_wait(last)

    def finish(j):
        near[j] = collapse(last, j, near[j])

    loop(0, targets, finish)

    for k in range(1, zs):
        own_copy(k).wait_recv()
    w_take().wait_recv()

    def project(pieces, which):
        width = wall.shape[-1]
        flat = pieces[...].reshape(zs * mid, BLK)
        first = wall[which, :, :mid, :].reshape(zs * mid, width)
        second = wall[which, :, mid:, :].reshape(zs * mid, width)
        return dot_tn(flat, first)[:HALF] + dot_tn(flat, second)[HALF:]

    self_part = project(own_r, 1) + bias_ref[...].reshape(1, -1)

    ring_wait(0, reach - 1)
    ring_wait(1, reach - 1)

    def agg_copy(dest):
        return to_feat(agg_s.at[dest], agg_r.at[z], agg_ss.at[dest], agg_rs.at[z], dest)

    for j in range(targets):
        total = near[j] + ring_in[0, reach - 1, j].astype(F32) + ring_in[1, reach - 1, j].astype(F32)
        degree = deg_ref[pl.ds(j * BLK, BLK)].reshape(1, BLK).astype(F32)
        block = (total / degree).astype(BF)
        agg_t[j] = block
        first, second = pack_halves(block)
        for half, piece in ((0, first), (1, second)):
            dest = 2 * j + half
            agg_s[dest] = piece

            @pl.when(z != dest)
            def _(dest=dest):
                agg_copy(dest).start()

            @pl.when(z == dest)
            def _(dest=dest, piece=piece):
                agg_r[dest] = piece

    def agg_wait(k):
        source = z_peer(k)
        to_feat(agg_s.at[source], agg_r.at[source], agg_ss.at[source], agg_rs.at[source], source).wait_recv()

    for k in range(1, zs):
        agg_wait(k)
    pre = project(agg_r, 0) + self_part

    scale = 0.7978845608028654
    cubic = 0.044715
    inner = jnp.tanh(scale * (pre + cubic * (pre * pre * pre)))
    cdf = 0.5 * (1.0 + inner)
    act_ref[...] = (pre * cdf).astype(BF)
    slope = cdf + pre * (0.5 * (1.0 - inner * inner)) * (scale * (1.0 + 3.0 * cubic * (pre * pre)))
    sl[z] = (cot_ref[...].astype(F32) * slope).astype(BF)

    def sl_copy(k):
        return to_feat(sl.at[z], sl.at[z], sl_ss.at[k], sl_rs.at[k], z_peer(k))

    for k in range(1, zs):
        sl_copy(k).start()
    for k in range(1, zs):
        sl_copy(k).wait_recv()

    width = sl.shape[-1]
    grad_n = jnp.zeros((fw, width), F32)
    grad_s = jnp.zeros((fw, width), F32)
    grad_b = jnp.zeros((8, width), F32)
    for j in range(targets):
        rows = sl[2 * j : 2 * j + 2].reshape(BLK, width)
        grad_n = grad_n + jnp.dot(agg_t[j], rows, preferred_element_type=F32)
        grad_s = grad_s + jnp.dot(own_t[j], rows, preferred_element_type=F32)
        grad_b = grad_b + rows.astype(F32).reshape(BLK // 8, 8, width).sum(axis=0)
    per = 4 * fw // row
    unit = mid
    share = ar_t.shape[0] // col

    def places():
        for u in range(8):
            yield u // 4, (u // 2) % 2, u % 2, u * unit // per, u * unit % per

    for which, side, part, owner, at in places():
        grad = (grad_n, grad_s)[which]
        ar_g[owner, at : at + unit] = grad[part * unit : (part + 1) * unit, side * BLK : (side + 1) * BLK]
    for owner in range(row):
        ar_g[owner, per : per + 8] = grad_b[:, :BLK]
        ar_g[owner, per + 8 : per + 16] = grad_b[:, BLK:]
        if ar_t.shape[0] > per + 16:
            ar_g[owner, per + 16 :] = jnp.zeros((ar_t.shape[0] - per - 16, BLK), F32)

    def a_copy(r):
        return to_node(ar_g.at[lax.rem(g + r, row)], ar_r.at[r], a_ss.at[r], a_rs.at[r], row_peer(r))

    for r in range(1, row):
        a_copy(r).start()
    total = ar_g[g]
    for r in range(1, row):
        a_copy(r).wait_recv()
        total = total + ar_r[r]
    ar_sum[...] = total

    def b_copy(k):
        rows = pl.ds(pl.multiple_of(lax.rem(y + k, col) * share, 8), share)
        return to_node(ar_sum.at[rows], ar_y.at[k], b_ss.at[k], b_rs.at[k], col_peer(k))

    for k in range(1, col):
        b_copy(k).start()
    mine = pl.ds(pl.multiple_of(y * share, 8), share)
    total = ar_sum[mine]
    for k in range(1, col):
        b_copy(k).wait_recv()
        total = total + ar_y[k]
    ar_t[mine] = total

    def c_copy(k):
        return to_node(ar_t.at[mine], ar_t.at[mine], c_ss.at[k], c_rs.at[k], col_peer(k))

    for k in range(1, col):
        c_copy(k).start()
    for k in range(1, col):
        c_copy(k).wait_recv()

    def d_copy(r):
        return to_node(ar_t, ar_full.at[g], d_ss.at[r], d_rs.at[r], row_peer(r))

    for r in range(1, row):
        d_copy(r).start()
    ar_full[g] = ar_t[...]
    for r in range(1, row):
        d_copy(r).wait_recv()

    for which, side, part, owner, at in places():
        out = (gn_ref, gs_ref)[which]
        out[part * unit : (part + 1) * unit, side * BLK : (side + 1) * BLK] = ar_full[owner, at : at + unit]
    gb_ref[:, :BLK] = ar_full[0, per : per + 8].sum(axis=0, keepdims=True)
    gb_ref[:, BLK:] = ar_full[0, per + 8 : per + 16].sum(axis=0, keepdims=True)

    def row_sent(p):
        for r in range(1, row):
            row_copy(r, p).wait_send()

    loop(0, col, row_sent)
    for side in range(2):
        ring_first(side).wait_send()
    for p in range(1, last):
        ring_copy(p).wait_send()
    w_hand().wait_send()
    for k in range(1, col):
        slot_copy(k).wait_send()
        b_copy(k).wait_send()
        c_copy(k).wait_send()
    for r in range(1, row):
        a_copy(r).wait_send()
        d_copy(r).wait_send()
    for k in range(1, zs):
        own_copy(k).wait_send()
        w_copy(k).wait_send()
        sl_copy(k).wait_send()
        agg_copy(z_peer(k)).wait_send()


def local(row, features, w_neigh, w_self, bias, target_blocks, loc_tiles, loc_src, loc_count, rem_tiles, rem_src,
          rem_slot, degree, cotangent):
    fw = features.shape[1]
    nblocks = features.shape[0] // BLK
    targets, slots = loc_src.shape
    nodes = lax.axis_size("nodes")
    zs = lax.axis_size("feat")
    col = nodes // row
    width = w_neigh.shape[1]
    mid = fw // 2
    per = 4 * fw // row
    chunk = -(-(per + 16) // (8 * col)) * 8 * col
    hbm = pl.BlockSpec(memory_space=pl.ANY)
    vmem = pl.BlockSpec(memory_space=pltpu.VMEM)
    smem = pl.BlockSpec(memory_space=pltpu.SMEM)
    dma = pltpu.SemaphoreType.DMA
    scratch = [
        pltpu.VMEM(features.shape, BF),
        pltpu.VMEM((nblocks, fw, BLK), BF),
        pltpu.VMEM((col, row, BLK, BLK), BF),
        pltpu.VMEM((targets, slots, BLK, BLK), BF),
        pltpu.VMEM((row, col, fw, BLK), BF),
        pltpu.VMEM((row, col, fw, BLK), BF),
        pltpu.VMEM((targets, fw, BLK), F32),
        pltpu.VMEM((targets, fw, BLK), F32),
        pltpu.VMEM((col, 8, BLK), jnp.int32),
        pltpu.SMEM((col, 8, BLK), jnp.int32),
        pltpu.VMEM((col - 1, targets, fw, BLK), BF),
        pltpu.VMEM((2, col // 2, targets, fw, BLK), BF),
        pltpu.VMEM((targets, fw, BLK), BF),
        pltpu.VMEM((targets, fw, BLK), BF),
        pltpu.VMEM((zs, mid, BLK), BF),
        pltpu.VMEM((zs, mid, BLK), BF),
        pltpu.VMEM((zs, mid, BLK), BF),
        pltpu.VMEM((zs, mid, BLK), BF),
        pltpu.VMEM((2, zs, fw, width), BF),
        pltpu.VMEM((zs, HALF, width), BF),
        pltpu.VMEM((row, chunk, BLK), F32),
        pltpu.VMEM((row, chunk, BLK), F32),
        pltpu.VMEM((chunk, BLK), F32),
        pltpu.VMEM((col, chunk // col, BLK), F32),
        pltpu.VMEM((chunk, BLK), F32),
        pltpu.VMEM((row, chunk, BLK), F32),
        dma((4,)), dma((col,)),
        dma((row, col)), dma((row, col)),
        dma((col,)), dma((col,)),
        dma((2, col // 2)), dma((2, col // 2)),
        dma((zs,)), dma((zs,)),
        dma((zs,)), dma((zs,)),
        dma((zs,)), dma((zs,)),
        dma((1,)), dma((1,)),
        dma((zs,)), dma((zs,)),
        dma((row,)), dma((row,)),
        dma((col,)), dma((col,)),
        dma((col,)), dma((col,)),
        dma((row,)), dma((row,)),
    ]
    activation, grad_neigh, grad_self, grad_bias = pl.pallas_call(
        functools.partial(kernel, row),
        out_shape=(
            jax.ShapeDtypeStruct(cotangent.shape, BF),
            jax.ShapeDtypeStruct(w_neigh.shape, F32),
            jax.ShapeDtypeStruct(w_self.shape, F32),
            jax.ShapeDtypeStruct((1, width), F32),
        ),
        in_specs=[hbm, hbm, hbm, vmem, smem, hbm, smem, smem, hbm, smem, vmem, vmem, vmem],
        out_specs=(vmem, vmem, vmem, vmem),
        scratch_shapes=scratch,
        compiler_params=pltpu.CompilerParams(
            collective_id=0, has_side_effects=True, vmem_limit_bytes=40 * 1024 * 1024
        ),
        name="sage_layer",
    )(features, w_neigh, w_self, bias, target_blocks, loc_tiles, loc_src, loc_count, rem_tiles, rem_src, rem_slot,
      degree, cotangent)
    return activation, grad_neigh, grad_self, grad_bias.reshape(width)


def solution(mesh, row=ROW_SIZE):
    return jax.shard_map(
        functools.partial(local, row),
        mesh=mesh,
        in_specs=(
            P("nodes", "feat"),
            P("feat", None),
            P("feat", None),
            P(),
            P("nodes"),
            P("nodes", None, None, None),
            P("nodes", None),
            P("nodes"),
            P("nodes", None, None, None),
            P("nodes", None),
            P("nodes", None),
            P("nodes"),
            P(("nodes", "feat"), None),
        ),
        out_specs=(P(("nodes", "feat"), None), P("feat", None), P("feat", None), P()),
        check_vma=False,
    )
```

```python
import functools

import jax
import jax.numpy as jnp
from jax import lax
from jax.experimental import pallas as pl
from jax.experimental.pallas import tpu as pltpu
from jax.sharding import PartitionSpec as P

BF = jnp.bfloat16
F32 = jnp.float32
MESH = pl.DeviceIdType.MESH
BLK = 128
HALF = 64
SLOPE_PHASES = (3, 3)
ROW_SIZE = 8


def dot_nt(a, b):
    return lax.dot_general(a, b, (((1,), (1,)), ((), ())), preferred_element_type=F32)


def dot_tn(a, b):
    return lax.dot_general(a, b, (((0,), (0,)), ((), ())), preferred_element_type=F32)


def loop(low, high, body):
    lax.fori_loop(low, high, lambda i, carry: (body(i), carry)[1], 0)


def pack_halves(block):
    mid = block.shape[0] // 2
    top, bottom = block[:mid], block[mid:]
    first = jnp.concatenate([top[:, :HALF], bottom[:, :HALF]], axis=1)
    second = jnp.concatenate([top[:, HALF:], bottom[:, HALF:]], axis=1)
    return first, second


def kernel(
    row,
    feat_hbm, wn_hbm, ws_hbm, bias_hbm, tb_hbm, loct_hbm, lsrc_hbm, lcnt_hbm, remt_hbm, rsrc_hbm, rslot_hbm, deg_hbm, cot_hbm,
    act_ref, full_ref,
    bias_ref, tb, lsrc, lcnt, rsrc, rslot, deg_ref, cot_ref,
    xt, remt, loct, sb, rb, near, pacc, slot_v, slot_m, ring_out, ring_in,
    own_t, agg_t, own_s, own_r, agg_s, agg_r, wall, sl,
    ar_g, ar_r, ar_y, ar_full,
    ld, ld_small, ld_feat, ld_rem, row_ss, row_rs, slot_ss, slot_rs, ring_ss, ring_rs,
    own_ss, own_rs, agg_ss, agg_rs, w_ss, w_rs, wc_ss, wc_rs, sl_ss, sl_rs,
    a_ss, a_rs, b_ss, b_rs, d_ss, d_rs,
):
    n = lax.axis_index("nodes")
    z = lax.axis_index("feat")
    nodes = lax.axis_size("nodes")
    zs = lax.axis_size("feat")
    col = nodes // row
    reach = col // 2
    last = col - 1
    y = lax.div(n, row)
    g = lax.rem(n, row)
    core = lax.rem(g, 2)
    targets = near.shape[0]
    fw = xt.shape[1]
    mid = fw // 2
    nblocks = xt.shape[0]

    def row_peer(r):
        return y * row + lax.rem(g + r, row)

    def col_peer(k):
        return lax.rem(y + k, col) * row + g

    def z_peer(k):
        return lax.rem(z + k, zs)

    def delta(p):
        return (reach - (p + 1) // 2) * (2 * (p % 2) - 1)

    def to_node(src, dst, ssem, rsem, node):
        return pltpu.make_async_remote_copy(
            src_ref=src, dst_ref=dst, send_sem=ssem, recv_sem=rsem, device_id={"nodes": node}, device_id_type=MESH
        )

    def to_feat(src, dst, ssem, rsem, peer):
        return pltpu.make_async_remote_copy(
            src_ref=src, dst_ref=dst, send_sem=ssem, recv_sem=rsem, device_id={"feat": peer}, device_id_type=MESH
        )

    def relay(buffer, rows, reaches, ssem, rsem):
        half = rows // 2
        base, phases = 0, []
        for reach_now in reaches:
            top = min(base + reach_now, zs // 2)
            phases.append((base, top))
            base = top

        def copy(side, dist, start):
            sign = 1 - 2 * side
            shard = lax.rem(z - sign * start + zs, zs)
            peer = lax.rem(z + sign * (dist - start) + zs, zs)
            part = pl.ds(side * half, half) if 2 * dist == zs else pl.ds(0, rows)
            ref = buffer.at[shard, part]
            return to_feat(ref, ref, ssem.at[side, dist], rsem.at[side, dist], peer)

        def phase(i):
            low, top = phases[i]
            for side in range(2):
                if low > 0:
                    copy(side, low, phases[i - 1][0]).wait_recv()
                for dist in range(top, low, -1):
                    copy(side, dist, low).start()

        def rest(wait_send):
            for low, top in phases:
                for dist in range(low + 1, top + 1):
                    for side in range(2):
                        if wait_send:
                            copy(side, dist, low).wait_send()
                        elif dist < top or dist == zs // 2:
                            copy(side, dist, low).wait_recv()

        return phase, rest

    barrier = pltpu.get_barrier_semaphore()
    for r in range(1, row):
        pl.semaphore_signal(barrier, inc=1, device_id={"nodes": row_peer(r)}, device_id_type=MESH)
    for k in range(1, col):
        pl.semaphore_signal(barrier, inc=1, device_id={"nodes": col_peer(k)}, device_id_type=MESH)
    for k in range(1, zs):
        pl.semaphore_signal(barrier, inc=1, device_id={"feat": z_peer(k)}, device_id_type=MESH)

    def load_feat(b):
        return pltpu.make_async_copy(feat_hbm.at[:, pl.ds(b * BLK, BLK)], xt.at[b], ld_feat.at[b])

    small = [
        pltpu.make_async_copy(src, dst, ld_small.at[i])
        for i, (src, dst) in enumerate(
            ((rsrc_hbm, rsrc), (tb_hbm, tb), (lsrc_hbm, lsrc), (lcnt_hbm, lcnt), (rslot_hbm, rslot), (deg_hbm, deg_ref),
             (cot_hbm, cot_ref), (bias_hbm, bias_ref))
        )
    ]
    small[0].start()
    for b in range(nblocks):
        load_feat(b).start()

    def dest_row(p):
        return lax.rem(y + delta(p) + col, col)

    def load_rem(p):
        return pltpu.make_async_copy(remt_hbm.at[0, pl.ds(dest_row(p) * row, row)], remt.at[p], ld_rem.at[p])

    for p in range(col):
        load_rem(p).start()
    for copy in small[1:]:
        copy.start()
    load_loc = pltpu.make_async_copy(loct_hbm, loct, ld.at[1])
    load_loc.start()
    load_wn = pltpu.make_async_copy(wn_hbm, wall.at[0, z], ld.at[2])
    load_ws = pltpu.make_async_copy(ws_hbm, wall.at[1, z], ld.at[2])

    @pl.when(core == 0)
    def _():
        load_wn.start()

    @pl.when(core == 1)
    def _():
        load_ws.start()

    small[0].wait()
    for b in range(nblocks):
        load_feat(b).wait()

    def messages(p):
        load_rem(p).wait()
        yd = dest_row(p)
        for r in range(row):
            gd = lax.rem(g + r, row)
            block = xt[rsrc[0, yd * row + gd]]
            message = dot_nt(block, remt[p, gd]).astype(BF)
            if r == 0:
                rb[0, p] = message
            else:
                sb[r, p] = message

    def row_copy(r, p):
        return to_node(sb.at[r, p], rb.at[r, p], row_ss.at[r, p], row_rs.at[r, p], row_peer(r))

    messages(0)
    slot_v[0] = jnp.zeros(slot_v.shape[1:], jnp.int32)
    small[4].wait()
    slot_v[0, 0:1, 0:nodes] = rslot[...]
    pl.semaphore_wait(barrier, row + col + zs - 3)

    def slot_copy(k):
        return to_node(slot_v.at[0], slot_v.at[k], slot_ss.at[k], slot_rs.at[k], col_peer(k))

    def own_copy(k):
        return to_feat(own_s.at[z_peer(k)], own_r.at[z], own_ss.at[k], own_rs.at[k], z_peer(k))

    w_phase, w_rest = relay(wall.at[core], fw, (3, 3), w_ss, w_rs)

    for r in range(1, row):
        row_copy(r, 0).start()
    for k in range(1, col):
        slot_copy(k).start()

    @pl.when(core == 0)
    def _():
        load_wn.wait()

    @pl.when(core == 1)
    def _():
        load_ws.wait()

    w_phase(0)

    def more(p):
        messages(p)
        for r in range(1, row):
            row_copy(r, p).start()

    loop(1, col, more)

    for copy in small[1:4] + small[5:]:
        copy.wait()
    for j in range(targets):
        block = xt[tb[j]]
        own_t[j] = block
        first, second = pack_halves(block)
        own_s[2 * j] = first
        own_s[2 * j + 1] = second
    own_r[z] = own_s[z]
    for k in range(1, zs):
        own_copy(k).start()

    load_loc.wait()

    def nearby(t):
        total = jnp.zeros((fw, BLK), F32)
        for k in range(lsrc.shape[1]):
            block = xt[lsrc[t, k]]
            block = jnp.where(k < lcnt[t], block, jnp.zeros_like(block))
            total = total + dot_nt(block, loct[t, k])
        near[t] = total

    loop(0, targets, nearby)


    for k in range(1, col):
        slot_copy(k).wait_recv()
    slots = pltpu.make_async_copy(slot_v, slot_m, ld.at[3])
    slots.start()
    slots.wait()

    def collapse(p, j, start):
        k = lax.rem(col - delta(p), col)
        total = start
        for r in range(row):
            source = y * row + lax.rem(g - r + row, row)
            hit = slot_m[k, 0, source] == j
            message = rb[r, p].astype(F32)
            total = total + jnp.where(hit, message, jnp.zeros_like(message))
        return total

    def row_wait(p):
        for r in range(1, row):
            row_copy(r, p).wait_recv()

    up = lax.rem(y + 1, col) * row + g
    down = lax.rem(y + col - 1, col) * row + g
    sides = (up, down)

    def ring_first(side):
        rows = pl.ds(side * mid, mid)
        return to_node(
            ring_out.at[0, :, rows], ring_in.at[side, 0, :, rows], ring_ss.at[side, 0], ring_rs.at[side, 0], sides[side]
        )

    def ring_copy(p):
        side, step = (p - 1) % 2, (p - 1) // 2 + 1
        return to_node(
            ring_out.at[p], ring_in.at[side, step], ring_ss.at[side, step], ring_rs.at[side, step], sides[side]
        )

    def ring_wait(side, step):
        if step == 0:
            ring_first(side).wait_recv()
        else:
            ring_copy(2 * step - 1 + side).wait_recv()

    row_wait(0)

    def start_ring(j):
        ring_out[0, j] = collapse(0, j, jnp.zeros((fw, BLK), F32)).astype(BF)

    loop(0, targets, start_ring)
    ring_first(0).start()
    ring_first(1).start()

    for p in range(1, last):
        side, step = (p - 1) % 2, (p - 1) // 2
        row_wait(p)

        def partial(j, p=p):
            pacc[j] = collapse(p, j, jnp.zeros((fw, BLK), F32))

        loop(0, targets, partial)
        ring_wait(side, step)

        def merge(j, p=p, side=side, step=step):
            if step == 0:
                own = pl.ds(side * mid, mid)
                other = pl.ds((1 - side) * mid, mid)
                ring_out[p, j, own] = (pacc[j, own] + ring_in[side, 0, j, own].astype(F32)).astype(BF)
                ring_out[p, j, other] = pacc[j, other].astype(BF)
            else:
                ring_out[p, j] = (pacc[j] + ring_in[side, step, j].astype(F32)).astype(BF)

        loop(0, targets, merge)
        ring_copy(p).start()
        if p == 2 and zs > 6:
            w_phase(1)

    partner = n + 1 - 2 * core

    def w_hand():
        return to_node(wall.at[core], wall.at[core], wc_ss.at[0], wc_rs.at[0], partner)

    def w_take():
        return to_node(wall.at[1 - core], wall.at[1 - core], wc_ss.at[0], wc_rs.at[0], partner)

    w_rest(False)
    w_hand().start()

    row_wait(last)

    def finish(j):
        near[j] = collapse(last, j, near[j])

    loop(0, targets, finish)

    for k in range(1, zs):
        own_copy(k).wait_recv()
    w_take().wait_recv()

    def project(pieces, which):
        width = wall.shape[-1]
        flat = pieces[...].reshape(zs * mid, BLK)
        first = wall[which, :, :mid, :].reshape(zs * mid, width)
        second = wall[which, :, mid:, :].reshape(zs * mid, width)
        return dot_tn(flat, first)[:HALF] + dot_tn(flat, second)[HALF:]

    self_part = project(own_r, 1) + bias_ref[...].reshape(1, -1)

    ring_wait(0, reach - 1)
    ring_wait(1, reach - 1)

    def agg_copy(dest):
        return to_feat(agg_s.at[dest], agg_r.at[z], agg_ss.at[dest], agg_rs.at[z], dest)

    for j in range(targets):
        total = near[j] + ring_in[0, reach - 1, j].astype(F32) + ring_in[1, reach - 1, j].astype(F32)
        degree = deg_ref[pl.ds(j * BLK, BLK)].reshape(1, BLK).astype(F32)
        block = (total / degree).astype(BF)
        agg_t[j] = block
        first, second = pack_halves(block)
        for half, piece in ((0, first), (1, second)):
            dest = 2 * j + half
            agg_s[dest] = piece

            @pl.when(z != dest)
            def _(dest=dest):
                agg_copy(dest).start()

            @pl.when(z == dest)
            def _(dest=dest, piece=piece):
                agg_r[dest] = piece

    def agg_wait(k):
        source = z_peer(k)
        to_feat(agg_s.at[source], agg_r.at[source], agg_ss.at[source], agg_rs.at[source], source).wait_recv()

    for k in range(1, zs):
        agg_wait(k)
    pre = project(agg_r, 0) + self_part

    scale = 0.7978845608028654
    cubic = 0.044715
    inner = jnp.tanh(scale * (pre + cubic * (pre * pre * pre)))
    cdf = 0.5 * (1.0 + inner)
    act_ref[...] = (pre * cdf).astype(BF)
    slope = cdf + pre * (0.5 * (1.0 - inner * inner)) * (scale * (1.0 + 3.0 * cubic * (pre * pre)))
    sl[z] = (cot_ref[...].astype(F32) * slope).astype(BF)

    sl_phase, sl_rest = relay(sl, HALF, SLOPE_PHASES, sl_ss, sl_rs)
    sl_phase(0)
    for i in range(1, len(SLOPE_PHASES)):
        if sum(SLOPE_PHASES[:i]) < zs // 2:
            sl_phase(i)
    sl_rest(False)

    width = sl.shape[-1]
    grad_n = jnp.zeros((fw, width), F32)
    grad_s = jnp.zeros((fw, width), F32)
    grad_b = jnp.zeros((8, width), F32)
    for j in range(targets):
        rows = sl[2 * j : 2 * j + 2].reshape(BLK, width)
        grad_n = grad_n + jnp.dot(agg_t[j], rows, preferred_element_type=F32)
        grad_s = grad_s + jnp.dot(own_t[j], rows, preferred_element_type=F32)
        grad_b = grad_b + rows.astype(F32).reshape(BLK // 8, 8, width).sum(axis=0)
    per = 4 * fw // row
    for which, side, part, owner, at in places(row, fw):
        unit = fw // 2
        grad = (grad_n, grad_s)[which]
        ar_g[owner, at : at + unit] = grad[part * unit : (part + 1) * unit, side * BLK : (side + 1) * BLK].astype(BF)
    bias_part = jnp.concatenate([grad_b[:, :BLK], grad_b[:, BLK:]], axis=0).astype(BF)
    for owner in range(row):
        ar_g[owner, per : per + 16] = bias_part

    def a_copy(r):
        return to_node(ar_g.at[lax.rem(g + r, row)], ar_r.at[r], a_ss.at[r], a_rs.at[r], row_peer(r))

    for r in range(1, row):
        a_copy(r).start()
    total = ar_g[g].astype(F32)
    for r in range(1, row):
        a_copy(r).wait_recv()
        total = total + ar_r[r].astype(F32)
    ar_y[y] = total.astype(BF)

    def b_copy(k):
        return to_node(ar_y.at[y], ar_y.at[y], b_ss.at[k], b_rs.at[k], col_peer(k))

    for k in range(1, col):
        b_copy(k).start()
    for k in range(1, col):
        b_copy(k).wait_recv()
    total = ar_y[0].astype(F32)
    for k in range(1, col):
        total = total + ar_y[k].astype(F32)
    ar_full[g] = total.astype(BF)

    def d_copy(r):
        return to_node(ar_full.at[g], ar_full.at[g], d_ss.at[r], d_rs.at[r], row_peer(r))

    for r in range(1, row):
        d_copy(r).start()
    for r in range(1, row):
        d_copy(r).wait_recv()
    full_ref[...] = ar_full[...]

    def row_sent(p):
        for r in range(1, row):
            row_copy(r, p).wait_send()

    loop(0, col, row_sent)
    for side in range(2):
        ring_first(side).wait_send()
    for p in range(1, last):
        ring_copy(p).wait_send()
    w_hand().wait_send()
    for k in range(1, col):
        slot_copy(k).wait_send()
        b_copy(k).wait_send()
    for r in range(1, row):
        a_copy(r).wait_send()
        d_copy(r).wait_send()
    for k in range(1, zs):
        own_copy(k).wait_send()
        agg_copy(z_peer(k)).wait_send()
    w_rest(True)
    sl_rest(True)


def places(row, fw):
    per, unit = 4 * fw // row, fw // 2
    for u in range(8):
        yield u // 4, (u // 2) % 2, u % 2, u * unit // per, u * unit % per


def hand_over_kernel(act, sums, act_out, gn_out, gs_out, gb_out):
    row, fw = sums.shape[0], gn_out.shape[0]
    unit, per = fw // 2, 4 * fw // row
    act_out[...] = act[...]
    for which, side, part, owner, at in places(row, fw):
        out = (gn_out, gs_out)[which]
        piece = sums[owner, at : at + unit].astype(F32)
        out[part * unit : (part + 1) * unit, side * BLK : (side + 1) * BLK] = piece
    rows = sums[0, per : per + 16].astype(F32)
    both = [rows[:8].sum(axis=0, keepdims=True), rows[8:].sum(axis=0, keepdims=True)]
    gb_out[...] = jnp.concatenate(both, axis=1).reshape(gb_out.shape)


def hand_over(activation, sums, fw, width):
    vmem = pl.BlockSpec(memory_space=pltpu.VMEM)
    return pl.pallas_call(
        hand_over_kernel,
        out_shape=(
            jax.ShapeDtypeStruct(activation.shape, BF),
            jax.ShapeDtypeStruct((fw, width), F32),
            jax.ShapeDtypeStruct((fw, width), F32),
            jax.ShapeDtypeStruct((width,), F32),
        ),
        in_specs=[vmem] * 2,
        out_specs=(vmem,) * 4,
        compiler_params=pltpu.CompilerParams(vmem_limit_bytes=56 * 1024 * 1024),
        name="hand_over",
    )(activation, sums)


def local(row, features, w_neigh, w_self, bias, target_blocks, loc_tiles, loc_src, loc_count, rem_tiles, rem_src,
          rem_slot, degree, cotangent):
    fw = features.shape[1]
    nblocks = features.shape[0] // BLK
    targets, slots = loc_src.shape
    nodes = lax.axis_size("nodes")
    zs = lax.axis_size("feat")
    col = nodes // row
    width = w_neigh.shape[1]
    mid = fw // 2
    per = 4 * fw // row
    chunk = per + 16
    hbm = pl.BlockSpec(memory_space=pltpu.HBM)
    vmem = pl.BlockSpec(memory_space=pltpu.VMEM)
    dma = pltpu.SemaphoreType.DMA
    scratch = [
        pltpu.VMEM(bias.shape, F32),
        pltpu.SMEM(target_blocks.shape, jnp.int32),
        pltpu.SMEM(loc_src.shape, jnp.int32),
        pltpu.SMEM(loc_count.shape, jnp.int32),
        pltpu.SMEM(rem_src.shape, jnp.int32),
        pltpu.VMEM(rem_slot.shape, jnp.int32),
        pltpu.VMEM(degree.shape, jnp.int32),
        pltpu.VMEM(cotangent.shape, BF),
        pltpu.VMEM((nblocks, fw, BLK), BF),
        pltpu.VMEM((col, row, BLK, BLK), BF),
        pltpu.VMEM((targets, slots, BLK, BLK), BF),
        pltpu.VMEM((row, col, fw, BLK), BF),
        pltpu.VMEM((row, col, fw, BLK), BF),
        pltpu.VMEM((targets, fw, BLK), F32),
        pltpu.VMEM((targets, fw, BLK), F32),
        pltpu.VMEM((col, 8, BLK), jnp.int32),
        pltpu.SMEM((col, 8, BLK), jnp.int32),
        pltpu.VMEM((col - 1, targets, fw, BLK), BF),
        pltpu.VMEM((2, col // 2, targets, fw, BLK), BF),
        pltpu.VMEM((targets, fw, BLK), BF),
        pltpu.VMEM((targets, fw, BLK), BF),
        pltpu.VMEM((zs, mid, BLK), BF),
        pltpu.VMEM((zs, mid, BLK), BF),
        pltpu.VMEM((zs, mid, BLK), BF),
        pltpu.VMEM((zs, mid, BLK), BF),
        pltpu.VMEM((2, zs, fw, width), BF),
        pltpu.VMEM((zs, HALF, width), BF),
        pltpu.VMEM((row, chunk, BLK), BF),
        pltpu.VMEM((row, chunk, BLK), BF),
        pltpu.VMEM((col, chunk, BLK), BF),
        pltpu.VMEM((row, chunk, BLK), BF),
        dma((4,)), dma((8,)), dma((nblocks,)), dma((col,)),
        dma((row, col)), dma((row, col)),
        dma((col,)), dma((col,)),
        dma((2, col // 2)), dma((2, col // 2)),
        dma((zs,)), dma((zs,)),
        dma((zs,)), dma((zs,)),
        dma((2, zs // 2 + 1)), dma((2, zs // 2 + 1)),
        dma((1,)), dma((1,)),
        dma((2, zs // 2 + 1)), dma((2, zs // 2 + 1)),
        dma((row,)), dma((row,)),
        dma((col,)), dma((col,)),
        dma((row,)), dma((row,)),
    ]
    activation, sums = pl.pallas_call(
        functools.partial(kernel, row),
        out_shape=(
            jax.ShapeDtypeStruct(cotangent.shape, BF),
            jax.ShapeDtypeStruct((row, chunk, BLK), BF),
        ),
        in_specs=[hbm] * 13,
        out_specs=(vmem, vmem),
        scratch_shapes=scratch,
        compiler_params=pltpu.CompilerParams(
            collective_id=0, has_side_effects=True, vmem_limit_bytes=56 * 1024 * 1024
        ),
        name="sage_layer",
    )(features.T, w_neigh, w_self, bias, target_blocks, loc_tiles, loc_src, loc_count, rem_tiles, rem_src, rem_slot,
      degree, cotangent)
    return hand_over(activation, sums, fw, width)


def solution(mesh, row=ROW_SIZE):
    return jax.shard_map(
        functools.partial(local, row),
        mesh=mesh,
        in_specs=(
            P("nodes", "feat"),
            P("feat", None),
            P("feat", None),
            P(),
            P("nodes"),
            P("nodes", None, None, None),
            P("nodes", None),
            P("nodes"),
            P("nodes", None, None, None),
            P("nodes", None),
            P("nodes", None),
            P("nodes"),
            P(("nodes", "feat"), None),
        ),
        out_specs=(P(("nodes", "feat"), None), P("feat", None), P("feat", None), P()),
        check_vma=False,
    )
```

```python
import functools

import jax
import jax.numpy as jnp
from jax import lax
from jax.experimental import pallas as pl
from jax.experimental.pallas import tpu as pltpu
from jax.sharding import PartitionSpec as P

BF = jnp.bfloat16
F32 = jnp.float32
MESH = pl.DeviceIdType.MESH
BLK = 128
HALF = 64
SLOPE_PHASES = (3, 3)
FEED = 4
ROW_SIZE = 8


def dot_nt(a, b):
    return lax.dot_general(a, b, (((1,), (1,)), ((), ())), preferred_element_type=F32)


def dot_tn(a, b):
    return lax.dot_general(a, b, (((0,), (0,)), ((), ())), preferred_element_type=F32)


def loop(low, high, body):
    lax.fori_loop(low, high, lambda i, carry: (body(i), carry)[1], 0)


def pack_halves(block):
    mid = block.shape[0] // 2
    top, bottom = block[:mid], block[mid:]
    first = jnp.concatenate([top[:, :HALF], bottom[:, :HALF]], axis=1)
    second = jnp.concatenate([top[:, HALF:], bottom[:, HALF:]], axis=1)
    return first, second


def kernel(
    row,
    feat_hbm, wn_hbm, ws_hbm, bias_hbm, tb_hbm, loct_hbm, lsrc_hbm, lcnt_hbm, remt_hbm, rsrc_hbm, rslot_hbm, deg_hbm, cot_hbm,
    act_ref, full_ref,
    bias_ref, tb, lsrc, lcnt, rsrc, rslot, deg_ref, cot_ref,
    xt, remt, loct, sb, rb, near, slot_v, slot_m, ring_out, ring_in,
    own_t, agg_t, own_s, own_r, agg_s, agg_r, wall, sl,
    ar_g, ar_r, ar_y, ar_full,
    ld, ld_small, ld_feat, ld_rem, row_ss, row_rs, slot_ss, slot_rs, ring_ss, ring_rs,
    own_ss, own_rs, agg_ss, agg_rs, w_ss, w_rs, wc_ss, wc_rs, sl_ss, sl_rs,
    a_ss, a_rs, b_ss, b_rs, d_ss, d_rs,
):
    n = lax.axis_index("nodes")
    z = lax.axis_index("feat")
    nodes = lax.axis_size("nodes")
    zs = lax.axis_size("feat")
    col = nodes // row
    reach = col // 2
    last = col - 1
    y = lax.div(n, row)
    g = lax.rem(n, row)
    core = lax.rem(g, 2)
    targets = near.shape[0]
    fw = xt.shape[1]
    mid = fw // 2
    nblocks = xt.shape[0]
    groups = ring_rs.shape[2]
    group = targets // groups

    def row_peer(r):
        return y * row + lax.rem(g + r, row)

    def col_peer(k):
        return lax.rem(y + k, col) * row + g

    def z_peer(k):
        return lax.rem(z + k, zs)

    def delta(p):
        return (reach - (p + 1) // 2) * (2 * (p % 2) - 1)

    def to_node(src, dst, ssem, rsem, node):
        return pltpu.make_async_remote_copy(
            src_ref=src, dst_ref=dst, send_sem=ssem, recv_sem=rsem, device_id={"nodes": node}, device_id_type=MESH
        )

    def to_feat(src, dst, ssem, rsem, peer):
        return pltpu.make_async_remote_copy(
            src_ref=src, dst_ref=dst, send_sem=ssem, recv_sem=rsem, device_id={"feat": peer}, device_id_type=MESH
        )

    def relay(buffer, rows, reaches, ssem, rsem):
        half = rows // 2
        base, phases = 0, []
        for reach_now in reaches:
            top = min(base + reach_now, zs // 2)
            phases.append((base, top))
            base = top

        def copy(side, dist, start):
            sign = 1 - 2 * side
            shard = lax.rem(z - sign * start + zs, zs)
            peer = lax.rem(z + sign * (dist - start) + zs, zs)
            part = pl.ds(side * half, half) if 2 * dist == zs else pl.ds(0, rows)
            ref = buffer.at[shard, part]
            return to_feat(ref, ref, ssem.at[0], rsem.at[side, dist], peer)

        def phase(i):
            low, top = phases[i]
            for side in range(2):
                if low > 0:
                    copy(side, low, phases[i - 1][0]).wait_recv()
                for dist in range(top, low, -1):
                    copy(side, dist, low).start()

        def rest():
            for low, top in phases:
                for dist in range(low + 1, top + 1):
                    for side in range(2):
                        if dist < top or dist == zs // 2:
                            copy(side, dist, low).wait_recv()

        def sent():
            every = buffer.at[pl.ds(0, zs - 1)]
            to_feat(every, every, ssem.at[0], rsem.at[0, 1], z_peer(1)).wait_send()

        return phase, rest, sent

    def load_feat(b):
        return pltpu.make_async_copy(feat_hbm.at[:, pl.ds(b * BLK, BLK)], xt.at[b], ld_feat.at[0])

    small = [
        pltpu.make_async_copy(src, dst, ld_small.at[i])
        for i, (src, dst) in enumerate(
            ((rsrc_hbm, rsrc), (tb_hbm, tb), (lsrc_hbm, lsrc), (lcnt_hbm, lcnt), (rslot_hbm, rslot), (deg_hbm, deg_ref),
             (cot_hbm, cot_ref), (bias_hbm, bias_ref))
        )
    ]
    small[0].start()
    for b in range(nblocks):
        load_feat(b).start()

    def dest_row(p):
        return lax.rem(y + delta(p) + col, col)

    def load_rem(p):
        return pltpu.make_async_copy(remt_hbm.at[0, pl.ds(dest_row(p) * row, row)], remt.at[p], ld_rem.at[p])

    load_rem(0).start()

    barrier = pltpu.get_barrier_semaphore()
    for r in range(1, row):
        pl.semaphore_signal(barrier, inc=1, device_id={"nodes": row_peer(r)}, device_id_type=MESH)
    for k in range(1, col):
        pl.semaphore_signal(barrier, inc=1, device_id={"nodes": col_peer(k)}, device_id_type=MESH)
    for k in range(1, zs):
        pl.semaphore_signal(barrier, inc=1, device_id={"feat": z_peer(k)}, device_id_type=MESH)

    for p in range(1, col):
        load_rem(p).start()
    for copy in small[1:]:
        copy.start()
    load_loc = pltpu.make_async_copy(loct_hbm, loct, ld.at[1])
    load_loc.start()
    load_wn = pltpu.make_async_copy(wn_hbm, wall.at[0, z], ld.at[2])
    load_ws = pltpu.make_async_copy(ws_hbm, wall.at[1, z], ld.at[2])

    @pl.when(core == 0)
    def _():
        load_wn.start()

    @pl.when(core == 1)
    def _():
        load_ws.start()

    ring_in[0, 0, :, mid:] = jnp.zeros((targets, mid, BLK), BF)
    ring_in[1, 0, :, :mid] = jnp.zeros((targets, mid, BLK), BF)

    small[0].wait()
    pltpu.make_async_copy(xt, xt, ld_feat.at[0]).wait()

    def messages(p):
        load_rem(p).wait()
        yd = dest_row(p)
        for r in range(row):
            gd = lax.rem(g + r, row)
            block = xt[rsrc[0, yd * row + gd]]
            message = dot_nt(block, remt[p, gd]).astype(BF)
            if r == 0:
                rb[0, p] = message
            else:
                sb[r, p] = message

    def row_copy(r, p):
        return to_node(sb.at[r, p], rb.at[r, p], row_ss.at[0], row_rs.at[p], row_peer(r))

    messages(0)
    slot_v[0] = jnp.zeros(slot_v.shape[1:], jnp.int32)
    small[4].wait()
    slot_v[0, 0:1, 0:nodes] = rslot[...]
    pl.semaphore_wait(barrier, row + col + zs - 3)

    def slot_copy(k):
        return to_node(slot_v.at[0], slot_v.at[k], slot_ss.at[0], slot_rs.at[0], col_peer(k))

    def own_copy(k):
        return to_feat(own_s.at[z_peer(k)], own_r.at[z], own_ss.at[0], own_rs.at[0], z_peer(k))

    w_phase, w_rest, w_sent = relay(wall.at[core], fw, (3, 3), w_ss, w_rs)

    for k in range(1, col):
        slot_copy(k).start()
    for r in range(1, row):
        row_copy(r, 0).start()

    @pl.when(core == 0)
    def _():
        load_wn.wait()

    @pl.when(core == 1)
    def _():
        load_ws.wait()

    w_phase(0)

    def more(p):
        messages(p)
        for r in range(1, row):
            row_copy(r, p).start()

    early = min(FEED, last)
    loop(1, early, more)


    def nearby(t):
        total = jnp.zeros((fw, BLK), F32)
        for k in range(lsrc.shape[1]):
            block = xt[lsrc[t, k]]
            block = jnp.where(k < lcnt[t], block, jnp.zeros_like(block))
            total = total + dot_nt(block, loct[t, k])
        near[t] = total

    def slot_all():
        rest = slot_v.at[pl.ds(1, col - 1)]
        return to_node(rest, rest, slot_ss.at[0], slot_rs.at[0], col_peer(1))

    slot_all().wait_recv()
    slots = pltpu.make_async_copy(slot_v, slot_m, ld.at[3])
    slots.start()
    slots.wait()

    def collapse(p, j, start):
        k = lax.rem(col - delta(p), col)
        total = start
        for r in range(row):
            source = y * row + lax.rem(g - r + row, row)
            hit = slot_m[k, 0, source] == j
            message = rb[r, p].astype(F32)
            total = total + jnp.where(hit, message, jnp.zeros_like(message))
        return total

    def row_wait(p):
        others = pl.ds(1, row - 1)
        to_node(sb.at[others, p], rb.at[others, p], row_ss.at[0], row_rs.at[p], row_peer(1)).wait_recv()

    up = lax.rem(y + 1, col) * row + g
    down = lax.rem(y + col - 1, col) * row + g
    sides = (up, down)

    def ring_first(side, q):
        some, rows = pl.ds(q * group, group), pl.ds(side * mid, mid)
        return to_node(
            ring_out.at[0, some, rows],
            ring_in.at[side, 0, some, rows],
            ring_ss.at[0],
            ring_rs.at[side, 0, q],
            sides[side],
        )

    def ring_copy(p, q):
        side, step = (p - 1) % 2, (p - 1) // 2 + 1
        some = pl.ds(q * group, group)
        return to_node(
            ring_out.at[p, some],
            ring_in.at[side, step, some],
            ring_ss.at[0],
            ring_rs.at[side, step, q],
            sides[side],
        )

    def ring_wait(side, step, q):
        if step == 0:
            ring_first(side, q).wait_recv()
        else:
            ring_copy(2 * step - 1 + side, q).wait_recv()

    row_wait(0)

    def start_ring(q):
        for i in range(group):
            j = q * group + i
            ring_out[0, j] = collapse(0, j, jnp.zeros((fw, BLK), F32)).astype(BF)
        for side in range(2):
            ring_first(side, q).start()

    loop(0, groups, start_ring)
    loop(early, col, more)

    for copy in small[1:4] + small[5:]:
        copy.wait()
    for j in range(targets):
        block = xt[tb[j]]
        own_t[j] = block
        first, second = pack_halves(block)
        own_s[2 * j] = first
        own_s[2 * j + 1] = second
    own_r[z] = own_s[z]
    for k in range(1, zs):
        own_copy(k).start()

    load_loc.wait()

    for step in range(reach - 1):
        for side in range(2):
            p = 2 * step + 1 + side
            row_wait(p)

            def pass_on(q, p=p, side=side, step=step):
                parts = [collapse(p, q * group + i, jnp.zeros((fw, BLK), F32)) for i in range(group)]
                ring_wait(side, step, q)
                for i, part in enumerate(parts):
                    j = q * group + i
                    ring_out[p, j] = (part + ring_in[side, step, j].astype(F32)).astype(BF)
                ring_copy(p, q).start()

            loop(0, groups, pass_on)
        if step == 0 and zs > 6:
            w_phase(1)
        each = -(-targets // (reach - 1))
        loop(min(step * each, targets), min((step + 1) * each, targets), nearby)

    partner = n + 1 - 2 * core

    def w_hand():
        return to_node(wall.at[core], wall.at[core], wc_ss.at[0], wc_rs.at[0], partner)

    def w_take():
        return to_node(wall.at[1 - core], wall.at[1 - core], wc_ss.at[0], wc_rs.at[0], partner)

    w_rest()
    w_hand().start()

    row_wait(last)

    def finish(j):
        near[j] = collapse(last, j, near[j])

    loop(0, targets, finish)

    def own_all():
        rest = pl.ds(0, zs - 1)
        return to_feat(own_s.at[rest], own_r.at[rest], own_ss.at[0], own_rs.at[0], z_peer(1))

    own_all().wait_recv()
    w_take().wait_recv()

    def project(pieces, which):
        width = wall.shape[-1]
        flat = pieces[...].reshape(zs * mid, BLK)
        first = wall[which, :, :mid, :].reshape(zs * mid, width)
        second = wall[which, :, mid:, :].reshape(zs * mid, width)
        return dot_tn(flat, first)[:HALF] + dot_tn(flat, second)[HALF:]

    self_part = project(own_r, 1) + bias_ref[...].reshape(1, -1)

    def agg_copy(dest):
        return to_feat(agg_s.at[dest], agg_r.at[z], agg_ss.at[0], agg_rs.at[0], dest)

    for j in range(targets):
        if j % group == 0:
            ring_wait(0, reach - 1, j // group)
            ring_wait(1, reach - 1, j // group)
        total = near[j] + ring_in[0, reach - 1, j].astype(F32) + ring_in[1, reach - 1, j].astype(F32)
        degree = deg_ref[pl.ds(j * BLK, BLK)].reshape(1, BLK).astype(F32)
        block = (total / degree).astype(BF)
        agg_t[j] = block
        first, second = pack_halves(block)
        for half, piece in ((0, first), (1, second)):
            dest = 2 * j + half
            agg_s[dest] = piece

            @pl.when(z != dest)
            def _(dest=dest):
                agg_copy(dest).start()

            @pl.when(z == dest)
            def _(dest=dest, piece=piece):
                agg_r[dest] = piece

    def agg_all():
        rest = pl.ds(0, zs - 1)
        return to_feat(agg_s.at[rest], agg_r.at[rest], agg_ss.at[0], agg_rs.at[0], z_peer(1))

    agg_all().wait_recv()
    pre = project(agg_r, 0) + self_part

    scale = 0.7978845608028654
    cubic = 0.044715
    inner = jnp.tanh(scale * (pre + cubic * (pre * pre * pre)))
    cdf = 0.5 * (1.0 + inner)
    act_ref[...] = (pre * cdf).astype(BF)
    slope = cdf + pre * (0.5 * (1.0 - inner * inner)) * (scale * (1.0 + 3.0 * cubic * (pre * pre)))
    sl[z] = (cot_ref[...].astype(F32) * slope).astype(BF)

    sl_phase, sl_rest, sl_sent = relay(sl, HALF, SLOPE_PHASES, sl_ss, sl_rs)
    sl_phase(0)
    for i in range(1, len(SLOPE_PHASES)):
        if sum(SLOPE_PHASES[:i]) < zs // 2:
            sl_phase(i)
    sl_rest()

    width = sl.shape[-1]
    grad_n = jnp.zeros((fw, width), F32)
    grad_s = jnp.zeros((fw, width), F32)
    grad_b = jnp.zeros((8, width), F32)
    for j in range(targets):
        rows = sl[2 * j : 2 * j + 2].reshape(BLK, width)
        grad_n = grad_n + jnp.dot(agg_t[j], rows, preferred_element_type=F32)
        grad_s = grad_s + jnp.dot(own_t[j], rows, preferred_element_type=F32)
        grad_b = grad_b + rows.astype(F32).reshape(BLK // 8, 8, width).sum(axis=0)
    per = 4 * fw // row
    for which, side, part, owner, at in places(row, fw):
        unit = fw // 2
        grad = (grad_n, grad_s)[which]
        ar_g[owner, at : at + unit] = grad[part * unit : (part + 1) * unit, side * BLK : (side + 1) * BLK].astype(BF)
    bias_part = jnp.concatenate([grad_b[:, :BLK], grad_b[:, BLK:]], axis=0).astype(BF)
    for owner in range(row):
        ar_g[owner, per : per + 16] = bias_part

    others = pl.ds(1, row - 1)

    def a_copy(r):
        return to_node(ar_g.at[lax.rem(g + r, row)], ar_r.at[r], a_ss.at[0], a_rs.at[0], row_peer(r))

    for r in range(1, row):
        a_copy(r).start()
    total = ar_g[g].astype(F32)
    a_all = to_node(ar_g.at[others], ar_r.at[others], a_ss.at[0], a_rs.at[0], row_peer(1))
    a_all.wait_recv()
    for r in range(1, row):
        total = total + ar_r[r].astype(F32)
    ar_y[y] = total.astype(BF)

    def b_copy(k):
        return to_node(ar_y.at[y], ar_y.at[y], b_ss.at[0], b_rs.at[0], col_peer(k))

    for k in range(1, col):
        b_copy(k).start()
    b_rest = ar_y.at[pl.ds(0, col - 1)]
    b_all = to_node(b_rest, b_rest, b_ss.at[0], b_rs.at[0], col_peer(1))
    b_all.wait_recv()
    total = ar_y[0].astype(F32)
    for k in range(1, col):
        total = total + ar_y[k].astype(F32)
    ar_full[g] = total.astype(BF)

    def d_copy(r):
        return to_node(ar_full.at[g], ar_full.at[g], d_ss.at[0], d_rs.at[0], row_peer(r))

    for r in range(1, row):
        d_copy(r).start()
    d_rest = ar_full.at[pl.ds(0, row - 1)]
    d_all = to_node(d_rest, d_rest, d_ss.at[0], d_rs.at[0], row_peer(1))
    d_all.wait_recv()
    full_ref[...] = ar_full[...]

    to_node(sb.at[others], rb.at[others], row_ss.at[0], row_rs.at[0], row_peer(1)).wait_send()
    to_node(ring_out, ring_out, ring_ss.at[0], ring_rs.at[0, 0, 0], up).wait_send()
    w_hand().wait_send()
    slot_all().wait_send()
    own_all().wait_send()
    agg_all().wait_send()
    a_all.wait_send()
    b_all.wait_send()
    d_all.wait_send()
    w_sent()
    sl_sent()


def places(row, fw):
    per, unit = 4 * fw // row, fw // 2
    for u in range(8):
        yield u // 4, (u // 2) % 2, u % 2, u * unit // per, u * unit % per


def hand_over_kernel(act, sums, act_out, gn_out, gs_out, gb_out):
    row, fw = sums.shape[0], gn_out.shape[0]
    unit, per = fw // 2, 4 * fw // row
    act_out[...] = act[...]
    for which, side, part, owner, at in places(row, fw):
        out = (gn_out, gs_out)[which]
        piece = sums[owner, at : at + unit].astype(F32)
        out[part * unit : (part + 1) * unit, side * BLK : (side + 1) * BLK] = piece
    rows = sums[0, per : per + 16].astype(F32)
    both = [rows[:8].sum(axis=0, keepdims=True), rows[8:].sum(axis=0, keepdims=True)]
    gb_out[...] = jnp.concatenate(both, axis=1).reshape(gb_out.shape)


def hand_over(activation, sums, fw, width):
    vmem = pl.BlockSpec(memory_space=pltpu.VMEM)
    return pl.pallas_call(
        hand_over_kernel,
        out_shape=(
            jax.ShapeDtypeStruct(activation.shape, BF),
            jax.ShapeDtypeStruct((fw, width), F32),
            jax.ShapeDtypeStruct((fw, width), F32),
            jax.ShapeDtypeStruct((width,), F32),
        ),
        in_specs=[vmem] * 2,
        out_specs=(vmem,) * 4,
        compiler_params=pltpu.CompilerParams(vmem_limit_bytes=56 * 1024 * 1024),
        name="hand_over",
    )(activation, sums)


def local(row, features, w_neigh, w_self, bias, target_blocks, loc_tiles, loc_src, loc_count, rem_tiles, rem_src,
          rem_slot, degree, cotangent):
    fw = features.shape[1]
    nblocks = features.shape[0] // BLK
    targets, slots = loc_src.shape
    nodes = lax.axis_size("nodes")
    zs = lax.axis_size("feat")
    col = nodes // row
    width = w_neigh.shape[1]
    mid = fw // 2
    per = 4 * fw // row
    chunk = per + 16
    groups = 2 if targets % 2 == 0 else 1
    hbm = pl.BlockSpec(memory_space=pltpu.HBM)
    vmem = pl.BlockSpec(memory_space=pltpu.VMEM)
    dma = pltpu.SemaphoreType.DMA
    scratch = [
        pltpu.VMEM(bias.shape, F32),
        pltpu.SMEM(target_blocks.shape, jnp.int32),
        pltpu.SMEM(loc_src.shape, jnp.int32),
        pltpu.SMEM(loc_count.shape, jnp.int32),
        pltpu.SMEM(rem_src.shape, jnp.int32),
        pltpu.VMEM(rem_slot.shape, jnp.int32),
        pltpu.VMEM(degree.shape, jnp.int32),
        pltpu.VMEM(cotangent.shape, BF),
        pltpu.VMEM((nblocks, fw, BLK), BF),
        pltpu.VMEM((col, row, BLK, BLK), BF),
        pltpu.VMEM((targets, slots, BLK, BLK), BF),
        pltpu.VMEM((row, col, fw, BLK), BF),
        pltpu.VMEM((row, col, fw, BLK), BF),
        pltpu.VMEM((targets, fw, BLK), F32),
        pltpu.VMEM((col, 8, BLK), jnp.int32),
        pltpu.SMEM((col, 8, BLK), jnp.int32),
        pltpu.VMEM((col - 1, targets, fw, BLK), BF),
        pltpu.VMEM((2, col // 2, targets, fw, BLK), BF),
        pltpu.VMEM((targets, fw, BLK), BF),
        pltpu.VMEM((targets, fw, BLK), BF),
        pltpu.VMEM((zs, mid, BLK), BF),
        pltpu.VMEM((zs, mid, BLK), BF),
        pltpu.VMEM((zs, mid, BLK), BF),
        pltpu.VMEM((zs, mid, BLK), BF),
        pltpu.VMEM((2, zs, fw, width), BF),
        pltpu.VMEM((zs, HALF, width), BF),
        pltpu.VMEM((row, chunk, BLK), BF),
        pltpu.VMEM((row, chunk, BLK), BF),
        pltpu.VMEM((col, chunk, BLK), BF),
        pltpu.VMEM((row, chunk, BLK), BF),
        dma((4,)), dma((8,)), dma((1,)), dma((col,)),
        dma((1,)), dma((col,)),
        dma((1,)), dma((1,)),
        dma((1,)), dma((2, col // 2, groups)),
        dma((1,)), dma((1,)),
        dma((1,)), dma((1,)),
        dma((1,)), dma((2, zs // 2 + 1)),
        dma((1,)), dma((1,)),
        dma((1,)), dma((2, zs // 2 + 1)),
        dma((1,)), dma((1,)),
        dma((1,)), dma((1,)),
        dma((1,)), dma((1,)),
    ]
    activation, sums = pl.pallas_call(
        functools.partial(kernel, row),
        out_shape=(
            jax.ShapeDtypeStruct(cotangent.shape, BF),
            jax.ShapeDtypeStruct((row, chunk, BLK), BF),
        ),
        in_specs=[hbm] * 13,
        out_specs=(vmem, vmem),
        scratch_shapes=scratch,
        compiler_params=pltpu.CompilerParams(
            collective_id=0, has_side_effects=True, vmem_limit_bytes=56 * 1024 * 1024
        ),
        name="sage_layer",
    )(features.T, w_neigh, w_self, bias, target_blocks, loc_tiles, loc_src, loc_count, rem_tiles, rem_src, rem_slot,
      degree, cotangent)
    return hand_over(activation, sums, fw, width)


def solution(mesh, row=ROW_SIZE):
    return jax.shard_map(
        functools.partial(local, row),
        mesh=mesh,
        in_specs=(
            P("nodes", "feat"),
            P("feat", None),
            P("feat", None),
            P(),
            P("nodes"),
            P("nodes", None, None, None),
            P("nodes", None),
            P("nodes"),
            P("nodes", None, None, None),
            P("nodes", None),
            P("nodes", None),
            P("nodes"),
            P(("nodes", "feat"), None),
        ),
        out_specs=(P(("nodes", "feat"), None), P("feat", None), P("feat", None), P()),
        check_vma=False,
    )
```

```python
import functools

import jax
import jax.numpy as jnp
from jax import lax
from jax.experimental import pallas as pl
from jax.experimental.pallas import tpu as pltpu
from jax.sharding import PartitionSpec as P

BF = jnp.bfloat16
F32 = jnp.float32
MESH = pl.DeviceIdType.MESH
BLK = 128
HALF = 64
SLOPE_PHASES = (3, 3)
FEED = 4
ROW_SIZE = 8


def dot_nt(a, b):
    return lax.dot_general(a, b, (((1,), (1,)), ((), ())), preferred_element_type=F32)


def dot_tn(a, b):
    return lax.dot_general(a, b, (((0,), (0,)), ((), ())), preferred_element_type=F32)


def loop(low, high, body):
    lax.fori_loop(low, high, lambda i, carry: (body(i), carry)[1], 0)


def pack_halves(block):
    mid = block.shape[0] // 2
    top, bottom = block[:mid], block[mid:]
    first = jnp.concatenate([top[:, :HALF], bottom[:, :HALF]], axis=1)
    second = jnp.concatenate([top[:, HALF:], bottom[:, HALF:]], axis=1)
    return first, second


def kernel(
    row,
    feat_hbm, wn_hbm, ws_hbm, bias_hbm, tb_hbm, loct_hbm, lsrc_hbm, lcnt_hbm, remt_hbm, rsrc_hbm, rslot_hbm, deg_hbm, cot_hbm,
    act_ref, full_ref,
    bias_ref, tb, lsrc, lcnt, rsrc, rslot, deg_ref, cot_ref,
    xt, remt, loct, sb, rb, near, slot_v, slot_m, ring_out, ring_in,
    own_t, agg_t, own_s, own_r, agg_s, agg_r, wall, sl,
    ar_g, ar_r, ar_y, ar_full,
    ld, ld_small, ld_feat, ld_rem, row_ss, row_rs, slot_ss, slot_rs, ring_ss, ring_rs,
    own_ss, own_rs, agg_ss, agg_rs, w_ss, w_rs, wc_ss, wc_rs, sl_ss, sl_rs,
    a_ss, a_rs, b_ss, b_rs, d_ss, d_rs,
):
    n = lax.axis_index("nodes")
    z = lax.axis_index("feat")
    nodes = lax.axis_size("nodes")
    zs = lax.axis_size("feat")
    col = nodes // row
    reach = col // 2
    last = col - 1
    y = lax.div(n, row)
    g = lax.rem(n, row)
    core = lax.rem(g, 2)
    targets = near.shape[0]
    fw = xt.shape[1]
    mid = fw // 2
    nblocks = xt.shape[0]
    groups = ring_rs.shape[2]
    group = targets // groups

    def row_peer(r):
        return y * row + lax.rem(g + r, row)

    def col_peer(k):
        return lax.rem(y + k, col) * row + g

    def z_peer(k):
        return lax.rem(z + k, zs)

    def delta(p):
        return (reach - (p + 1) // 2) * (2 * (p % 2) - 1)

    def to_node(src, dst, ssem, rsem, node):
        return pltpu.make_async_remote_copy(
            src_ref=src, dst_ref=dst, send_sem=ssem, recv_sem=rsem, device_id={"nodes": node}, device_id_type=MESH
        )

    def to_feat(src, dst, ssem, rsem, peer):
        return pltpu.make_async_remote_copy(
            src_ref=src, dst_ref=dst, send_sem=ssem, recv_sem=rsem, device_id={"feat": peer}, device_id_type=MESH
        )

    def relay(buffer, rows, reaches, ssem, rsem):
        half = rows // 2
        base, phases = 0, []
        for reach_now in reaches:
            top = min(base + reach_now, zs // 2)
            phases.append((base, top))
            base = top

        def copy(side, dist, start):
            sign = 1 - 2 * side
            shard = lax.rem(z - sign * start + zs, zs)
            peer = lax.rem(z + sign * (dist - start) + zs, zs)
            part = pl.ds(side * half, half) if 2 * dist == zs else pl.ds(0, rows)
            ref = buffer.at[shard, part]
            return to_feat(ref, ref, ssem.at[0], rsem.at[side, dist], peer)

        def phase(i):
            low, top = phases[i]
            for side in range(2):
                if low > 0:
                    copy(side, low, phases[i - 1][0]).wait_recv()
                for dist in range(top, low, -1):
                    copy(side, dist, low).start()

        def rest():
            for low, top in phases:
                for dist in range(low + 1, top + 1):
                    for side in range(2):
                        if dist < top or dist == zs // 2:
                            copy(side, dist, low).wait_recv()

        def sent():
            every = buffer.at[pl.ds(0, zs - 1)]
            to_feat(every, every, ssem.at[0], rsem.at[0, 1], z_peer(1)).wait_send()

        return phase, rest, sent

    def load_feat(b):
        return pltpu.make_async_copy(feat_hbm.at[:, pl.ds(b * BLK, BLK)], xt.at[b], ld_feat.at[0])

    small = [
        pltpu.make_async_copy(src, dst, ld_small.at[i])
        for i, (src, dst) in enumerate(
            ((rsrc_hbm, rsrc), (tb_hbm, tb), (lsrc_hbm, lsrc), (lcnt_hbm, lcnt), (rslot_hbm, rslot), (deg_hbm, deg_ref),
             (cot_hbm, cot_ref), (bias_hbm, bias_ref))
        )
    ]
    small[0].start()
    for b in range(nblocks):
        load_feat(b).start()

    def dest_row(p):
        return lax.rem(y + delta(p) + col, col)

    def load_rem(p):
        return pltpu.make_async_copy(remt_hbm.at[0, pl.ds(dest_row(p) * row, row)], remt.at[p], ld_rem.at[p])

    load_rem(0).start()

    barrier = pltpu.get_barrier_semaphore()
    for r in range(1, row):
        pl.semaphore_signal(barrier, inc=1, device_id={"nodes": row_peer(r)}, device_id_type=MESH)
    for k in range(1, col):
        pl.semaphore_signal(barrier, inc=1, device_id={"nodes": col_peer(k)}, device_id_type=MESH)
    for k in range(1, zs):
        pl.semaphore_signal(barrier, inc=1, device_id={"feat": z_peer(k)}, device_id_type=MESH)

    for p in range(1, col):
        load_rem(p).start()
    for copy in small[1:]:
        copy.start()
    load_loc = pltpu.make_async_copy(loct_hbm, loct, ld.at[1])
    load_loc.start()
    load_wn = pltpu.make_async_copy(wn_hbm, wall.at[0, z], ld.at[2])
    load_ws = pltpu.make_async_copy(ws_hbm, wall.at[1, z], ld.at[2])

    @pl.when(core == 0)
    def _():
        load_wn.start()

    @pl.when(core == 1)
    def _():
        load_ws.start()

    ring_in[0, 0, :, mid:] = jnp.zeros((targets, mid, BLK), BF)
    ring_in[1, 0, :, :mid] = jnp.zeros((targets, mid, BLK), BF)

    small[0].wait()
    pltpu.make_async_copy(xt, xt, ld_feat.at[0]).wait()

    def messages(p):
        load_rem(p).wait()
        yd = dest_row(p)
        for r in range(row):
            gd = lax.rem(g + r, row)
            block = xt[rsrc[0, yd * row + gd]]
            message = dot_nt(block, remt[p, gd]).astype(BF)
            if r == 0:
                rb[0, p] = message
            else:
                sb[r, p] = message

    def row_copy(r, p):
        return to_node(sb.at[r, p], rb.at[r, p], row_ss.at[0], row_rs.at[p], row_peer(r))

    messages(0)
    slot_v[0] = jnp.zeros(slot_v.shape[1:], jnp.int32)
    small[4].wait()
    slot_v[0, 0:1, 0:nodes] = rslot[...]
    pl.semaphore_wait(barrier, row + col + zs - 3)

    def slot_copy(k):
        return to_node(slot_v.at[0], slot_v.at[k], slot_ss.at[0], slot_rs.at[0], col_peer(k))

    def own_copy(k):
        return to_feat(own_s.at[z_peer(k)], own_r.at[z], own_ss.at[0], own_rs.at[0], z_peer(k))

    w_phase, w_rest, w_sent = relay(wall.at[core], fw, (3, 3), w_ss, w_rs)

    for k in range(1, col):
        slot_copy(k).start()
    for r in range(1, row):
        row_copy(r, 0).start()

    @pl.when(core == 0)
    def _():
        load_wn.wait()

    @pl.when(core == 1)
    def _():
        load_ws.wait()

    w_phase(0)

    def more(p):
        messages(p)
        for r in range(1, row):
            row_copy(r, p).start()

    early = min(FEED, last)
    loop(1, early, more)


    def nearby(t):
        total = jnp.zeros((fw, BLK), F32)
        for k in range(lsrc.shape[1]):
            block = xt[lsrc[t, k]]
            block = jnp.where(k < lcnt[t], block, jnp.zeros_like(block))
            total = total + dot_nt(block, loct[t, k])
        near[t] = total

    def slot_all():
        rest = slot_v.at[pl.ds(1, col - 1)]
        return to_node(rest, rest, slot_ss.at[0], slot_rs.at[0], col_peer(1))

    slot_all().wait_recv()
    slots = pltpu.make_async_copy(slot_v, slot_m, ld.at[3])
    slots.start()
    slots.wait()

    def collapse(p, j, start):
        k = lax.rem(col - delta(p), col)
        total = start
        for r in range(row):
            source = y * row + lax.rem(g - r + row, row)
            hit = slot_m[k, 0, source] == j
            message = rb[r, p].astype(F32)
            total = total + jnp.where(hit, message, jnp.zeros_like(message))
        return total

    def row_wait(p):
        others = pl.ds(1, row - 1)
        to_node(sb.at[others, p], rb.at[others, p], row_ss.at[0], row_rs.at[p], row_peer(1)).wait_recv()

    up = lax.rem(y + 1, col) * row + g
    down = lax.rem(y + col - 1, col) * row + g
    sides = (up, down)

    def ring_first(side, q):
        some, rows = pl.ds(q * group, group), pl.ds(side * mid, mid)
        return to_node(
            ring_out.at[0, some, rows],
            ring_in.at[side, 0, some, rows],
            ring_ss.at[0],
            ring_rs.at[side, 0, q],
            sides[side],
        )

    def ring_copy(p, q):
        side, step = (p - 1) % 2, (p - 1) // 2 + 1
        some = pl.ds(q * group, group)
        return to_node(
            ring_out.at[p, some],
            ring_in.at[side, step, some],
            ring_ss.at[0],
            ring_rs.at[side, step, q],
            sides[side],
        )

    def ring_wait(side, step, q):
        if step == 0:
            ring_first(side, q).wait_recv()
        else:
            ring_copy(2 * step - 1 + side, q).wait_recv()

    row_wait(0)

    def start_ring(q):
        for i in range(group):
            j = q * group + i
            ring_out[0, j] = collapse(0, j, jnp.zeros((fw, BLK), F32)).astype(BF)
        for side in range(2):
            ring_first(side, q).start()

    loop(0, groups, start_ring)
    loop(early, col, more)

    for copy in small[1:4] + small[5:]:
        copy.wait()
    for j in range(targets):
        block = xt[tb[j]]
        own_t[j] = block
        first, second = pack_halves(block)
        own_s[2 * j] = first
        own_s[2 * j + 1] = second
    own_r[z] = own_s[z]
    for k in range(1, zs):
        own_copy(k).start()

    load_loc.wait()

    for step in range(reach - 1):
        for side in range(2):
            p = 2 * step + 1 + side
            row_wait(p)

            def pass_on(q, p=p, side=side, step=step):
                parts = [collapse(p, q * group + i, jnp.zeros((fw, BLK), F32)) for i in range(group)]
                ring_wait(side, step, q)
                for i, part in enumerate(parts):
                    j = q * group + i
                    ring_out[p, j] = (part + ring_in[side, step, j].astype(F32)).astype(BF)
                ring_copy(p, q).start()

            loop(0, groups, pass_on)
        if step == 0 and zs > 6:
            w_phase(1)
        each = -(-targets // (reach - 1))
        loop(min(step * each, targets), min((step + 1) * each, targets), nearby)

    partner = n + 1 - 2 * core

    def w_hand():
        return to_node(wall.at[core], wall.at[core], wc_ss.at[0], wc_rs.at[0], partner)

    def w_take():
        return to_node(wall.at[1 - core], wall.at[1 - core], wc_ss.at[0], wc_rs.at[0], partner)

    w_rest()
    w_hand().start()

    row_wait(last)

    def finish(j):
        near[j] = collapse(last, j, near[j])

    loop(0, targets, finish)

    def own_all():
        rest = pl.ds(0, zs - 1)
        return to_feat(own_s.at[rest], own_r.at[rest], own_ss.at[0], own_rs.at[0], z_peer(1))

    own_all().wait_recv()
    w_take().wait_recv()

    def project(pieces, which):
        width = wall.shape[-1]
        flat = pieces[...].reshape(zs * mid, BLK)
        first = wall[which, :, :mid, :].reshape(zs * mid, width)
        second = wall[which, :, mid:, :].reshape(zs * mid, width)
        return dot_tn(flat, first)[:HALF] + dot_tn(flat, second)[HALF:]

    self_part = project(own_r, 1) + bias_ref[...].reshape(1, -1)

    def agg_copy(dest):
        return to_feat(agg_s.at[dest], agg_r.at[z], agg_ss.at[0], agg_rs.at[0], dest)

    for j in range(targets):
        if j % group == 0:
            ring_wait(0, reach - 1, j // group)
            ring_wait(1, reach - 1, j // group)
        total = near[j] + ring_in[0, reach - 1, j].astype(F32) + ring_in[1, reach - 1, j].astype(F32)
        degree = deg_ref[pl.ds(j * BLK, BLK)].reshape(1, BLK).astype(F32)
        block = (total / degree).astype(BF)
        agg_t[j] = block
        first, second = pack_halves(block)
        for half, piece in ((0, first), (1, second)):
            dest = 2 * j + half
            agg_s[dest] = piece

            @pl.when(z != dest)
            def _(dest=dest):
                agg_copy(dest).start()

            @pl.when(z == dest)
            def _(dest=dest, piece=piece):
                agg_r[dest] = piece

    def agg_all():
        rest = pl.ds(0, zs - 1)
        return to_feat(agg_s.at[rest], agg_r.at[rest], agg_ss.at[0], agg_rs.at[0], z_peer(1))

    agg_all().wait_recv()
    pre = project(agg_r, 0) + self_part

    scale = 0.7978845608028654
    cubic = 0.044715
    inner = jnp.tanh(scale * (pre + cubic * (pre * pre * pre)))
    cdf = 0.5 * (1.0 + inner)
    act_ref[...] = (pre * cdf).astype(BF)
    slope = cdf + pre * (0.5 * (1.0 - inner * inner)) * (scale * (1.0 + 3.0 * cubic * (pre * pre)))
    sl[z] = (cot_ref[...].astype(F32) * slope).astype(BF)

    sl_phase, sl_rest, sl_sent = relay(sl, HALF, SLOPE_PHASES, sl_ss, sl_rs)
    sl_phase(0)
    for i in range(1, len(SLOPE_PHASES)):
        if sum(SLOPE_PHASES[:i]) < zs // 2:
            sl_phase(i)
    sl_rest()

    width = sl.shape[-1]
    grad_n = jnp.zeros((fw, width), F32)
    grad_s = jnp.zeros((fw, width), F32)
    grad_b = jnp.zeros((8, width), F32)
    for j in range(targets):
        rows = sl[2 * j : 2 * j + 2].reshape(BLK, width)
        grad_n = grad_n + jnp.dot(agg_t[j], rows, preferred_element_type=F32)
        grad_s = grad_s + jnp.dot(own_t[j], rows, preferred_element_type=F32)
        grad_b = grad_b + rows.astype(F32).reshape(BLK // 8, 8, width).sum(axis=0)
    per = 4 * fw // row
    for which, side, part, owner, at in places(row, fw):
        unit = fw // 2
        grad = (grad_n, grad_s)[which]
        ar_g[owner, at : at + unit] = grad[part * unit : (part + 1) * unit, side * BLK : (side + 1) * BLK].astype(BF)
    bias_part = jnp.concatenate([grad_b[:, :BLK], grad_b[:, BLK:]], axis=0).astype(BF)
    for owner in range(row):
        ar_g[owner, per : per + 16] = bias_part

    others = pl.ds(1, row - 1)

    def a_copy(r):
        return to_node(ar_g.at[lax.rem(g + r, row)], ar_r.at[g], a_ss.at[0], a_rs.at[0], row_peer(r))

    for r in range(1, row):
        a_copy(r).start()
    ar_r[g] = ar_g[g]
    a_all = to_node(ar_g.at[others], ar_r.at[others], a_ss.at[0], a_rs.at[0], row_peer(1))
    a_all.wait_recv()
    total = ar_r[0].astype(F32)
    for r in range(1, row):
        total = total + ar_r[r].astype(F32)
    ar_y[y] = total.astype(BF)

    def b_copy(k):
        return to_node(ar_y.at[y], ar_y.at[y], b_ss.at[0], b_rs.at[0], col_peer(k))

    for k in range(1, col):
        b_copy(k).start()
    b_rest = ar_y.at[pl.ds(0, col - 1)]
    b_all = to_node(b_rest, b_rest, b_ss.at[0], b_rs.at[0], col_peer(1))
    b_all.wait_recv()
    total = ar_y[0].astype(F32)
    for k in range(1, col):
        total = total + ar_y[k].astype(F32)
    ar_full[g, :per] = total[:per].astype(BF)

    for r in range(row):
        full_ref[r, per:] = total[per:].astype(BF)

    def d_copy(r):
        return to_node(ar_full.at[g, pl.ds(0, per)], ar_full.at[g, pl.ds(0, per)], d_ss.at[0], d_rs.at[0], row_peer(r))

    for r in range(1, row):
        d_copy(r).start()
    d_rest = ar_full.at[pl.ds(0, row - 1), pl.ds(0, per)]
    d_all = to_node(d_rest, d_rest, d_ss.at[0], d_rs.at[0], row_peer(1))
    d_all.wait_recv()
    full_ref[:, :per] = ar_full[:, :per]

    to_node(sb.at[others], rb.at[others], row_ss.at[0], row_rs.at[0], row_peer(1)).wait_send()
    to_node(ring_out, ring_out, ring_ss.at[0], ring_rs.at[0, 0, 0], up).wait_send()
    w_hand().wait_send()
    slot_all().wait_send()
    own_all().wait_send()
    agg_all().wait_send()
    a_all.wait_send()
    b_all.wait_send()
    d_all.wait_send()
    w_sent()
    sl_sent()


def places(row, fw):
    per, unit = 4 * fw // row, fw // 2
    for u in range(8):
        yield u // 4, (u // 2) % 2, u % 2, u * unit // per, u * unit % per


def hand_over_kernel(act, sums, act_out, gn_out, gs_out, gb_out):
    row, fw = sums.shape[0], gn_out.shape[0]
    unit, per = fw // 2, 4 * fw // row
    act_out[...] = act[...]
    for which, side, part, owner, at in places(row, fw):
        out = (gn_out, gs_out)[which]
        piece = sums[owner, at : at + unit].astype(F32)
        out[part * unit : (part + 1) * unit, side * BLK : (side + 1) * BLK] = piece
    rows = sums[0, per : per + 16].astype(F32)
    both = [rows[:8].sum(axis=0, keepdims=True), rows[8:].sum(axis=0, keepdims=True)]
    gb_out[...] = jnp.concatenate(both, axis=1).reshape(gb_out.shape)


def hand_over(activation, sums, fw, width):
    vmem = pl.BlockSpec(memory_space=pltpu.VMEM)
    return pl.pallas_call(
        hand_over_kernel,
        out_shape=(
            jax.ShapeDtypeStruct(activation.shape, BF),
            jax.ShapeDtypeStruct((fw, width), F32),
            jax.ShapeDtypeStruct((fw, width), F32),
            jax.ShapeDtypeStruct((width,), F32),
        ),
        in_specs=[vmem] * 2,
        out_specs=(vmem,) * 4,
        compiler_params=pltpu.CompilerParams(vmem_limit_bytes=56 * 1024 * 1024),
        name="hand_over",
    )(activation, sums)


def local(row, features, w_neigh, w_self, bias, target_blocks, loc_tiles, loc_src, loc_count, rem_tiles, rem_src,
          rem_slot, degree, cotangent):
    fw = features.shape[1]
    nblocks = features.shape[0] // BLK
    targets, slots = loc_src.shape
    nodes = lax.axis_size("nodes")
    zs = lax.axis_size("feat")
    col = nodes // row
    width = w_neigh.shape[1]
    mid = fw // 2
    per = 4 * fw // row
    chunk = per + 16
    groups = 2 if targets % 2 == 0 else 1
    hbm = pl.BlockSpec(memory_space=pltpu.HBM)
    vmem = pl.BlockSpec(memory_space=pltpu.VMEM)
    dma = pltpu.SemaphoreType.DMA
    scratch = [
        pltpu.VMEM(bias.shape, F32),
        pltpu.SMEM(target_blocks.shape, jnp.int32),
        pltpu.SMEM(loc_src.shape, jnp.int32),
        pltpu.SMEM(loc_count.shape, jnp.int32),
        pltpu.SMEM(rem_src.shape, jnp.int32),
        pltpu.VMEM(rem_slot.shape, jnp.int32),
        pltpu.VMEM(degree.shape, jnp.int32),
        pltpu.VMEM(cotangent.shape, BF),
        pltpu.VMEM((nblocks, fw, BLK), BF),
        pltpu.VMEM((col, row, BLK, BLK), BF),
        pltpu.VMEM((targets, slots, BLK, BLK), BF),
        pltpu.VMEM((row, col, fw, BLK), BF),
        pltpu.VMEM((row, col, fw, BLK), BF),
        pltpu.VMEM((targets, fw, BLK), F32),
        pltpu.VMEM((col, 8, BLK), jnp.int32),
        pltpu.SMEM((col, 8, BLK), jnp.int32),
        pltpu.VMEM((col - 1, targets, fw, BLK), BF),
        pltpu.VMEM((2, col // 2, targets, fw, BLK), BF),
        pltpu.VMEM((targets, fw, BLK), BF),
        pltpu.VMEM((targets, fw, BLK), BF),
        pltpu.VMEM((zs, mid, BLK), BF),
        pltpu.VMEM((zs, mid, BLK), BF),
        pltpu.VMEM((zs, mid, BLK), BF),
        pltpu.VMEM((zs, mid, BLK), BF),
        pltpu.VMEM((2, zs, fw, width), BF),
        pltpu.VMEM((zs, HALF, width), BF),
        pltpu.VMEM((row, chunk, BLK), BF),
        pltpu.VMEM((row, chunk, BLK), BF),
        pltpu.VMEM((col, chunk, BLK), BF),
        pltpu.VMEM((row, chunk, BLK), BF),
        dma((4,)), dma((8,)), dma((1,)), dma((col,)),
        dma((1,)), dma((col,)),
        dma((1,)), dma((1,)),
        dma((1,)), dma((2, col // 2, groups)),
        dma((1,)), dma((1,)),
        dma((1,)), dma((1,)),
        dma((1,)), dma((2, zs // 2 + 1)),
        dma((1,)), dma((1,)),
        dma((1,)), dma((2, zs // 2 + 1)),
        dma((1,)), dma((1,)),
        dma((1,)), dma((1,)),
        dma((1,)), dma((1,)),
    ]
    activation, sums = pl.pallas_call(
        functools.partial(kernel, row),
        out_shape=(
            jax.ShapeDtypeStruct(cotangent.shape, BF),
            jax.ShapeDtypeStruct((row, chunk, BLK), BF),
        ),
        in_specs=[hbm] * 13,
        out_specs=(vmem, vmem),
        scratch_shapes=scratch,
        compiler_params=pltpu.CompilerParams(
            collective_id=0, has_side_effects=True, vmem_limit_bytes=56 * 1024 * 1024
        ),
        name="sage_layer",
    )(features.T, w_neigh, w_self, bias, target_blocks, loc_tiles, loc_src, loc_count, rem_tiles, rem_src, rem_slot,
      degree, cotangent)
    return hand_over(activation, sums, fw, width)


def solution(mesh, row=ROW_SIZE):
    return jax.shard_map(
        functools.partial(local, row),
        mesh=mesh,
        in_specs=(
            P("nodes", "feat"),
            P("feat", None),
            P("feat", None),
            P(),
            P("nodes"),
            P("nodes", None, None, None),
            P("nodes", None),
            P("nodes"),
            P("nodes", None, None, None),
            P("nodes", None),
            P("nodes", None),
            P("nodes"),
            P(("nodes", "feat"), None),
        ),
        out_specs=(P(("nodes", "feat"), None), P("feat", None), P("feat", None), P()),
        check_vma=False,
    )
```
